32 devices in a mesh: tm: 8 (over z, y), patch: 4 (over x, core).
Axes of the slice: x: 2, y: 2, z: 4, core: 2. Of those that a mesh axis runs over, the one named last changes fastest.
Arguments:
- tokens: bfloat16 [64, 256, 768], P('tm', 'patch'), may hold values from -5 to 5
- time_gain: float32 [768], replicated, may hold values from 0.25 to 1.75
- time_proj: bfloat16 [768, 2304], replicated, may hold values from -1 to 1
- time_out: bfloat16 [768, 768], replicated, may hold values from -0.375 to 0.375
- time_scale: float32 [12], replicated, may hold values from 2 to 260
- space_gain: float32 [768], replicated, may hold values from 0.25 to 1.75
- space_proj: bfloat16 [768, 2304], replicated, may hold values from -1 to 1
- space_out: bfloat16 [768, 768], replicated, may hold values from -0.375 to 0.375
- space_scale: float32 [12], replicated, may hold values from 2 to 260
Outputs:
- block_out: bfloat16 [64, 256, 768], P('tm', 'patch')
The draws below stay inside these ranges and needn't reach their ends.
All inputs are finite; a program needn't handle non-finite values.
Results may differ from the reference program's by a relative error of at most 0.012.
The reference program's roundings to bfloat16 on the way count: a program that leaves them out, or rounds other values in their place, can miss the bound.
Values may be sent and summed in bfloat16 or wider, within the bound.
No kernel may reach another device: no remote copies, remote signals or barrier semaphores. Data moves between devices by JAX's collectives and lax.ppermute only.
A program may use at most 128 MiB of HBM per device.

```python
import jax
import jax.numpy as jnp
from jax import lax

D = 768
HEADS = 12
HEAD_DIM = 64
FR_DEV = 8
FRAMES = 64
PATCHES = 256


def mix_fields(key, tied):
    first, second = jax.random.split(key, 2)
    base = jnp.clip(jax.random.normal(first, (D, 3, D), jnp.float32), -4.0, 4.0)
    extra = jnp.clip(jax.random.normal(second, (D, D), jnp.float32), -4.0, 4.0)
    key_part = tied * (base[:, 0] + 0.1 * extra) / jnp.sqrt(1.01) + base[:, 1]
    stacked = jnp.stack([base[:, 0], key_part, base[:, 2]], axis=1)
    return (stacked.reshape(D, 3 * D) * D ** (-0.5)).astype(jnp.bfloat16)


def log_scales(key, lowest, highest):
    pick_key, spread_key = jax.random.split(key, 2)
    uniform_part = jax.random.uniform(spread_key, (HEADS,), jnp.float32)
    values = jnp.exp(jnp.log(lowest) + uniform_part * (jnp.log(highest) - jnp.log(lowest)))
    chosen = jax.random.randint(pick_key, (), 0, HEADS)
    indices = jnp.arange(HEADS)
    values = jnp.where(indices == chosen, highest, values)
    values = jnp.where(indices == (chosen + 1) % HEADS, lowest, values)
    return values.astype(jnp.float32)


def draw_tokens(key, part):
    key = jax.random.fold_in(key, 11)
    noise_key = jax.random.fold_in(key, 0)
    noise = jax.random.normal(noise_key, (FRAMES, PATCHES, D), jnp.float32)
    values = noise
    return jnp.clip(values, -5.0, 5.0).astype(jnp.bfloat16)


def draw_time_proj(key, part):
    key = jax.random.fold_in(key, 23)
    return mix_fields(key, 0.0)


def draw_space_proj(key, part):
    key = jax.random.fold_in(key, 37)
    return mix_fields(key, 0.0)


def draw_time_scale(key, part):
    key = jax.random.fold_in(key, 41)
    return log_scales(key, 6.0, 48.0)


def draw_space_scale(key, part):
    key = jax.random.fold_in(key, 53)
    return log_scales(key, 6.0, 48.0)


def bell_draw(own_key, shape, scale, reach, kind=jnp.bfloat16):
    return jnp.clip(scale * jax.random.normal(own_key, shape, jnp.float32), -reach, reach).astype(kind)


def setup_inputs(seed: int = 0) -> dict:
    key_list = jax.random.split(jax.random.key(seed), 10)
    return {
        "tokens": draw_tokens(jax.random.fold_in(key_list[9], 71), 0),
        "time_gain": jnp.clip(1.0 + 0.15 * jax.random.normal(key_list[1], (D,), jnp.float32), 0.25, 1.75),
        "time_proj": draw_time_proj(jax.random.fold_in(key_list[9], 71), 0),
        "time_out": bell_draw(key_list[3], (D, D), (4 * HEAD_DIM) ** -0.5, 0.375),
        "time_scale": draw_time_scale(jax.random.fold_in(key_list[9], 71), 0),
        "space_gain": jnp.clip(1.0 + 0.15 * jax.random.normal(key_list[5], (D,), jnp.float32), 0.25, 1.75),
        "space_proj": draw_space_proj(jax.random.fold_in(key_list[9], 71), 0),
        "space_out": bell_draw(key_list[7], (D, D), (4 * HEAD_DIM) ** -0.5, 0.375),
        "space_scale": draw_space_scale(jax.random.fold_in(key_list[9], 71), 0),
    }


EPSILON = 1e-06

def widen(values):
    return lax.optimization_barrier(values).astype(jnp.float32)

def layer_norm(values, gain_vector):
    widened = values.astype(jnp.float32)
    centred = widened - lax.optimization_barrier(jnp.mean(widened, axis=-1, keepdims=True))
    spread = lax.optimization_barrier(jnp.mean(centred * centred, axis=-1, keepdims=True))
    return (centred * lax.rsqrt(spread + EPSILON) * gain_vector).astype(jnp.bfloat16)

def project(normed, weight):
    flat = normed.reshape(-1, normed.shape[-1])
    fields = jnp.dot(flat, weight, preferred_element_type=jnp.float32)
    pieces = fields.reshape(fields.shape[:-1] + (3, HEADS, HEAD_DIM))
    paired = pieces[:, :2]
    paired = paired * lax.rsqrt(lax.optimization_barrier(jnp.sum(paired * paired, axis=-1, keepdims=True)) + EPSILON)
    joined = jnp.concatenate([paired, pieces[:, 2:]], axis=1)
    return joined.reshape(normed.shape[:-1] + (3 * HEADS * HEAD_DIM,)).astype(jnp.bfloat16)

def softmax_weights(scores):
    largest = lax.optimization_barrier(jnp.max(scores, axis=-1, keepdims=True))
    powers = jnp.exp(scores - largest)
    totals = lax.optimization_barrier(jnp.sum(powers, axis=-1, keepdims=True))
    return (widen(powers.astype(jnp.bfloat16)), totals)

def time_patch(column, time_gain, time_proj, time_out, time_scale):
    fields = project(layer_norm(column, time_gain), time_proj)
    pieces = widen(fields).reshape(FRAMES, 3, HEADS, HEAD_DIM)
    scores = jnp.einsum('qhd,khd->hqk', pieces[:, 0], pieces[:, 1]) * time_scale[:, None, None]
    weights, totals = softmax_weights(scores)
    attended = jnp.einsum('hqk,khd->qhd', weights, pieces[:, 2]) / jnp.swapaxes(totals, 0, 1)
    attended = attended.astype(jnp.bfloat16).reshape(FRAMES, HEADS * HEAD_DIM)
    update = jnp.dot(attended, time_out, preferred_element_type=jnp.float32)
    return (column.astype(jnp.float32) + update).astype(jnp.bfloat16)

def space_block(block, space_gain, space_proj, space_out, space_scale):
    fields = project(layer_norm(block, space_gain), space_proj)
    pieces = widen(fields).reshape(FR_DEV, PATCHES, 3, HEADS, HEAD_DIM)
    scores = jnp.einsum('fqhd,fkhd->fhqk', pieces[:, :, 0], pieces[:, :, 1]) * space_scale[None, :, None, None]
    weights, totals = softmax_weights(scores)
    attended = jnp.einsum('fhqk,fkhd->fqhd', weights, pieces[:, :, 2]) / jnp.swapaxes(totals, 1, 2)
    attended = attended.astype(jnp.bfloat16).reshape(FR_DEV * PATCHES, HEADS * HEAD_DIM)
    update = jnp.dot(attended, space_out, preferred_element_type=jnp.float32).reshape(block.shape)
    return (block.astype(jnp.float32) + update).astype(jnp.bfloat16)

def reference(tokens, time_gain, time_proj, time_out, time_scale, space_gain, space_proj, space_out, space_scale):
    columns = jnp.swapaxes(tokens, 0, 1)
    stream = lax.map(lambda column: time_patch(column, time_gain, time_proj, time_out, time_scale), columns)
    stream = jnp.swapaxes(stream, 0, 1)
    blocks = stream.reshape(FRAMES // FR_DEV, FR_DEV, PATCHES, HEADS * HEAD_DIM)
    result = lax.map(lambda block: space_block(block, space_gain, space_proj, space_out, space_scale), blocks)
    return result.reshape(FRAMES, PATCHES, HEADS * HEAD_DIM)
```

```python
import functools
import math

import jax
import jax.numpy as jnp
from jax import lax
from jax.experimental import pallas as pl
from jax.experimental.pallas import tpu as pltpu
from jax.sharding import PartitionSpec as P

HEADS = 12
HEAD_DIM = 64
WIDTH = HEADS * HEAD_DIM
EPSILON = 1e-06
LOG2_E = math.log2(math.e)
LANES = 128
GROUP = 256

NT = (((1,), (1,)), ((), ()))
TN = (((0,), (0,)), ((), ()))


def dot(left, right, dims=(((1,), (0,)), ((), ()))):
    return lax.dot_general(left, right, dims, preferred_element_type=jnp.float32)


def layer_norm(values, gain):
    centred = values - jnp.mean(values, axis=-1, keepdims=True)
    spread = jnp.mean(centred * centred, axis=-1, keepdims=True)
    return (centred * lax.rsqrt(spread + EPSILON) * gain).astype(jnp.bfloat16)


def unit_rows(fields):
    squares = jnp.sum(fields * fields, axis=0, keepdims=True)
    return (fields * lax.rsqrt(squares + EPSILON)).astype(jnp.bfloat16)


def hold(held, values):
    for part in range(held.shape[0]):
        held[part] = values[:, part * LANES : (part + 1) * LANES].astype(jnp.float32)


def pick(held, start, count, step):
    return jnp.concatenate(
        [held[part, pl.ds(start, count, stride=step), :] for part in range(held.shape[0])], axis=1
    )


def attend(keys, queries, values, factor, packed):
    scores = dot(keys, queries, TN)
    columns = scores.shape[1]
    if packed == 1:
        powers = jnp.exp2((scores - jnp.max(scores, axis=0, keepdims=True)) * factor)
        totals = jnp.sum(powers, axis=0, keepdims=True)
        weights = powers.astype(jnp.bfloat16)
    else:
        length = columns // packed
        owner = lax.broadcasted_iota(jnp.int32, (length, columns), 1) // length
        own = scores[:length]
        for item in range(1, packed):
            own = jnp.where(owner == item, scores[item * length : (item + 1) * length], own)
        powers = jnp.exp2((own - jnp.max(own, axis=0, keepdims=True)) * factor)
        totals = jnp.sum(powers, axis=0, keepdims=True)
        weights = jnp.concatenate(
            [jnp.where(owner == item, powers, 0.0).astype(jnp.bfloat16) for item in range(packed)], axis=0
        )
    return (dot(values, weights) * (1.0 / totals)).astype(jnp.bfloat16)


def attend_heads(normed, proj_ref, scale_ref, mixed_ref, span, packed):
    rows = normed.shape[0]
    for head in range(HEADS):
        low = head * HEAD_DIM
        queries = unit_rows(dot(proj_ref[low : low + HEAD_DIM], normed, NT))
        keys = unit_rows(dot(proj_ref[WIDTH + low : WIDTH + low + HEAD_DIM], normed, NT))
        values = dot(proj_ref[2 * WIDTH + low : 2 * WIDTH + low + HEAD_DIM], normed, NT).astype(jnp.bfloat16)
        factor = scale_ref[head] * LOG2_E
        for start in range(0, rows, span):
            cut = slice(start, start + span)
            mixed_ref[low : low + HEAD_DIM, cut] = attend(
                keys[:, cut], queries[:, cut], values[:, cut], factor, packed
            )


def time_kernel(frames, scale_ref, tokens_ref, gain_ref, proj_ref, out_ref, stream_ref, held, result, mixed):
    rows = tokens_ref.shape[0]
    patches = rows // frames
    together = max(1, min(patches, GROUP // frames))
    packed = max(1, min(together, LANES // frames))
    hold(held, tokens_ref)
    for first in range(0, patches, together):
        tokens = jnp.concatenate(
            [pick(held, first + item, frames, patches) for item in range(together)], axis=0
        )
        normed = layer_norm(tokens, gain_ref[...])
        attend_heads(normed, proj_ref, scale_ref, mixed, packed * frames, packed)
        stream = tokens + dot(mixed[...], out_ref[...], TN)
        for item in range(together):
            for part in range(result.shape[0]):
                result[part, pl.ds(first + item, frames, stride=patches), :] = stream[
                    item * frames : (item + 1) * frames, part * LANES : (part + 1) * LANES
                ]
    for part in range(result.shape[0]):
        stream_ref[:, part * LANES : (part + 1) * LANES] = result[part].astype(jnp.bfloat16)


def space_kernel(senders, sides, scale_ref, stream_ref, gain_ref, proj_ref, out_ref, block_ref, held, mixed):
    rows = stream_ref.shape[0]
    frames, all_patches = block_ref.shape[1], sides * block_ref.shape[2]
    piece = rows // senders // frames
    hold(held, stream_ref)
    for frame in range(frames):
        parts = []
        for side in range(sides):
            if piece % 8:
                start = (side * frames + frame) * piece
                parts.append(pick(held, start, senders // sides, sides * frames))
            else:
                for sender in range(side, senders, sides):
                    parts.append(pick(held, (sender * frames + frame) * piece, piece, 1))
        stream = jnp.concatenate(parts, axis=0)
        normed = layer_norm(stream, gain_ref[...])
        attend_heads(normed, proj_ref, scale_ref, mixed, all_patches, 1)
        block = (stream + dot(mixed[...], out_ref[...], TN)).astype(jnp.bfloat16)
        for side in range(sides):
            block_ref[side, frame] = block[side * (all_patches // sides) : (side + 1) * (all_patches // sides)]


def call(kernel, out_shape, scratch, scale, rows, gain, proj, out):
    whole = pl.BlockSpec(memory_space=pltpu.VMEM)
    return pl.pallas_call(
        kernel,
        out_shape=jax.ShapeDtypeStruct(out_shape, jnp.bfloat16),
        in_specs=[pl.BlockSpec(memory_space=pltpu.SMEM)] + [whole] * 4,
        out_specs=whole,
        scratch_shapes=scratch,
        compiler_params=pltpu.CompilerParams(vmem_limit_bytes=40 * 1024 * 1024),
        cost_estimate=pl.CostEstimate(flops=3 * 10**9, bytes_accessed=7 * 10**6, transcendentals=10**6),
    )(scale, rows, gain.reshape(1, -1), proj, out)


def per_device(
    tokens,
    time_gain,
    time_proj,
    time_out,
    time_scale,
    space_gain,
    space_proj,
    space_out,
    space_scale,
):
    frames, local_count, width = tokens.shape
    peers, sides = lax.axis_size("tm"), lax.axis_size("patch")
    rows = frames * local_count
    all_frames = frames * peers
    time_rows = max(GROUP, all_frames)
    outgoing = tokens.reshape(frames, peers, local_count // peers, width)
    outgoing = jnp.swapaxes(outgoing, 0, 1).reshape(peers, rows // peers, width)
    arrived = lax.all_to_all(outgoing, "tm", split_axis=0, concat_axis=0, tiled=True).reshape(rows, width)
    stream = call(
        functools.partial(time_kernel, all_frames),
        (rows, width),
        [
            pltpu.VMEM((width // LANES, rows, LANES), jnp.float32),
            pltpu.VMEM((width // LANES, rows, LANES), jnp.float32),
            pltpu.VMEM((width, time_rows), jnp.bfloat16),
        ],
        time_scale, arrived, time_gain, time_proj.T, time_out,
    )
    senders = peers * sides
    stream = lax.all_to_all(
        stream.reshape(senders, rows // senders, width), ("tm", "patch"), split_axis=0, concat_axis=0, tiled=True
    ).reshape(rows, width)
    block = call(
        functools.partial(space_kernel, senders, sides),
        (sides, frames // sides, local_count, width),
        [pltpu.VMEM((width // LANES, rows, LANES), jnp.float32), pltpu.VMEM((width, sides * local_count), jnp.bfloat16)],
        space_scale, stream, space_gain, space_proj.T, space_out,
    )
    block = lax.all_to_all(block, "patch", split_axis=0, concat_axis=0, tiled=True)
    return block.reshape(frames, local_count, width)


def solution(mesh):
    in_specs = (P("tm", "patch", None), P(), P(), P(), P(), P(), P(), P(), P())
    out_specs = P("tm", "patch", None)
    return jax.shard_map(
        per_device, mesh=mesh, in_specs=in_specs, out_specs=out_specs, check_vma=False
    )
```

```python
import functools
import math

import jax
import jax.numpy as jnp
from jax import lax
from jax.experimental import pallas as pl
from jax.experimental.pallas import tpu as pltpu
from jax.sharding import PartitionSpec as P

HEADS = 12
HEAD_DIM = 64
WIDTH = HEADS * HEAD_DIM
EPSILON = 1e-06
LOG2_E = math.log2(math.e)
LANES = 128

TN = (((0,), (0,)), ((), ()))
TT = (((0,), (1,)), ((), ()))


def dot(left, right, dims=(((1,), (0,)), ((), ()))):
    return lax.dot_general(left, right, dims, preferred_element_type=jnp.float32)


def layer_norm(values, gain):
    centred = values - jnp.mean(values, axis=-1, keepdims=True)
    spread = jnp.mean(centred * centred, axis=-1, keepdims=True)
    return (centred * lax.rsqrt(spread + EPSILON) * gain).astype(jnp.bfloat16)


def unit_columns(fields):
    heads = fields.reshape(HEADS, HEAD_DIM, fields.shape[1])
    squares = jnp.sum(heads * heads, axis=1, keepdims=True)
    return (heads * lax.rsqrt(squares + EPSILON)).reshape(fields.shape)


def project(normed, proj_ref, fields_ref):
    for part in range(3):
        cut = slice(part * WIDTH, (part + 1) * WIDTH)
        fields = dot(proj_ref[:, cut], normed, TT)
        if part < 2:
            fields = unit_columns(fields)
        fields_ref[cut] = fields.astype(jnp.bfloat16)


def hold(held, values):
    for part in range(held.shape[0]):
        held[part] = values[:, part * LANES : (part + 1) * LANES].astype(jnp.float32)


def pick(held, start, count, step):
    return jnp.concatenate(
        [held[part, pl.ds(start, count, stride=step), :] for part in range(held.shape[0])], axis=1
    )


def head_rows(part, head):
    return slice(part * WIDTH + head * HEAD_DIM, part * WIDTH + (head + 1) * HEAD_DIM)


def attend(fields_ref, scale_ref, mixed_ref, scores_ref, weights_ref, totals_ref, span, packed):
    length = span // packed
    owner = lax.broadcasted_iota(jnp.int32, (length, span), 1) // length
    for start in range(0, fields_ref.shape[1], span):
        cut = slice(start, start + span)
        for head in range(HEADS):
            scores_ref[head] = dot(fields_ref[head_rows(1, head), cut], fields_ref[head_rows(0, head), cut], TN)
        for head in range(HEADS):
            factor = scale_ref[head] * LOG2_E
            for low in range(0, span, LANES):
                lanes = slice(low, low + LANES)
                mine = owner[:, lanes]
                items = range(low // length, (low + LANES - 1) // length + 1) if packed > 1 else range(1)
                scores = scores_ref[head, items[0] * length : (items[0] + 1) * length, lanes]
                for item in items[1:]:
                    scores = jnp.where(mine == item, scores_ref[head, item * length : (item + 1) * length, lanes], scores)
                powers = jnp.exp2((scores - jnp.max(scores, axis=0, keepdims=True)) * factor)
                totals_ref[head, :, lanes] = 1.0 / jnp.sum(powers, axis=0, keepdims=True)
                for item in range(packed):
                    part = powers if packed == 1 else jnp.where(mine == item, powers, 0.0)
                    weights_ref[head, item * length : (item + 1) * length, lanes] = part.astype(jnp.bfloat16)
        for head in range(HEADS):
            mixed = dot(fields_ref[head_rows(2, head), cut], weights_ref[head]) * totals_ref[head]
            mixed_ref[head_rows(0, head), cut] = mixed.astype(jnp.bfloat16)


def time_kernel(
    frames, scale_ref, tokens_ref, gain_ref, proj_ref, out_ref, stream_ref, held, result, fields, mixed, *work
):
    patches = tokens_ref.shape[0] // frames
    span, packed = time_span(frames, patches)
    hold(held, tokens_ref)
    tokens = jnp.concatenate([pick(held, patch, frames, patches) for patch in range(patches)], axis=0)
    project(layer_norm(tokens, gain_ref[...]), proj_ref, fields)
    attend(fields, scale_ref, mixed, *work, span, packed)
    update = dot(mixed[...], out_ref[...], TN)
    for patch in range(patches):
        stream = pick(held, patch, frames, patches) + update[patch * frames : (patch + 1) * frames]
        for part in range(result.shape[0]):
            result[part, pl.ds(patch, frames, stride=patches), :] = stream[:, part * LANES : (part + 1) * LANES]
    for part in range(result.shape[0]):
        stream_ref[:, part * LANES : (part + 1) * LANES] = result[part].astype(jnp.bfloat16)


def space_kernel(
    senders, sides, scale_ref, stream_ref, gain_ref, proj_ref, out_ref, block_ref, held, fields, mixed, *work
):
    frames, side_patches = block_ref.shape[1:3]
    piece = stream_ref.shape[0] // senders // frames
    hold(held, stream_ref)

    def ordered():
        parts = []
        for frame in range(frames):
            for side in range(sides):
                if piece % 8:
                    start = (side * frames + frame) * piece
                    parts.append(pick(held, start, senders // sides, sides * frames))
                else:
                    for sender in range(side, senders, sides):
                        parts.append(pick(held, (sender * frames + frame) * piece, piece, 1))
        return jnp.concatenate(parts, axis=0)

    project(layer_norm(ordered(), gain_ref[...]), proj_ref, fields)
    attend(fields, scale_ref, mixed, *work, sides * side_patches, 1)
    block = (ordered() + dot(mixed[...], out_ref[...], TN)).astype(jnp.bfloat16)
    for frame in range(frames):
        for side in range(sides):
            start = (frame * sides + side) * side_patches
            block_ref[side, frame] = block[start : start + side_patches]


def time_span(frames, patches):
    packed = max(1, min(patches, LANES // frames))
    return packed * frames, packed


def work_space(rows, span):
    return [
        pltpu.VMEM((3 * WIDTH, rows), jnp.bfloat16),
        pltpu.VMEM((WIDTH, rows), jnp.bfloat16),
        pltpu.VMEM((HEADS, span, span), jnp.float32),
        pltpu.VMEM((HEADS, span, span), jnp.bfloat16),
        pltpu.VMEM((HEADS, 1, span), jnp.float32),
    ]


def call(kernel, out_shape, scratch, scale, rows, gain, proj, out):
    whole = pl.BlockSpec(memory_space=pltpu.VMEM)
    return pl.pallas_call(
        kernel,
        out_shape=jax.ShapeDtypeStruct(out_shape, jnp.bfloat16),
        in_specs=[pl.BlockSpec(memory_space=pltpu.SMEM)] + [whole] * 4,
        out_specs=whole,
        scratch_shapes=scratch,
        compiler_params=pltpu.CompilerParams(vmem_limit_bytes=40 * 1024 * 1024),
        cost_estimate=pl.CostEstimate(flops=3 * 10**9, bytes_accessed=7 * 10**6, transcendentals=10**6),
    )(scale, rows, gain.reshape(1, -1), proj, out)


def per_device(
    tokens,
    time_gain,
    time_proj,
    time_out,
    time_scale,
    space_gain,
    space_proj,
    space_out,
    space_scale,
):
    frames, local_count, width = tokens.shape
    peers, sides = lax.axis_size("tm"), lax.axis_size("patch")
    rows = frames * local_count
    all_frames = frames * peers
    outgoing = tokens.reshape(frames, peers, local_count // peers, width)
    outgoing = jnp.swapaxes(outgoing, 0, 1).reshape(peers, rows // peers, width)
    arrived = lax.all_to_all(outgoing, "tm", split_axis=0, concat_axis=0, tiled=True).reshape(rows, width)
    held = pltpu.VMEM((width // LANES, rows, LANES), jnp.float32)
    stream = call(
        functools.partial(time_kernel, all_frames),
        (rows, width),
        [held, held] + work_space(rows, time_span(all_frames, local_count // peers)[0]),
        time_scale, arrived, time_gain, time_proj, time_out,
    )
    senders = peers * sides
    stream = lax.all_to_all(
        stream.reshape(senders, rows // senders, width), ("tm", "patch"), split_axis=0, concat_axis=0, tiled=True
    ).reshape(rows, width)
    block = call(
        functools.partial(space_kernel, senders, sides),
        (sides, frames // sides, local_count, width),
        [held] + work_space(rows, sides * local_count),
        space_scale, stream, space_gain, space_proj, space_out,
    )
    block = lax.all_to_all(block, "patch", split_axis=0, concat_axis=0, tiled=True)
    return block.reshape(frames, local_count, width)


def solution(mesh):
    in_specs = (P("tm", "patch", None), P(), P(), P(), P(), P(), P(), P(), P())
    out_specs = P("tm", "patch", None)
    return jax.shard_map(
        per_device, mesh=mesh, in_specs=in_specs, out_specs=out_specs, check_vma=False
    )
```

```python
import functools
import math

import jax
import jax.numpy as jnp
from jax import lax
from jax.experimental import pallas as pl
from jax.experimental.pallas import tpu as pltpu
from jax.sharding import PartitionSpec as P

HEADS = 12
HEAD_DIM = 64
WIDTH = HEADS * HEAD_DIM
EPSILON = 1e-06
LOG2_E = math.log2(math.e)
LANES = 128
VMEM_BYTES = 24 * 1024 * 1024

TN = (((0,), (0,)), ((), ()))
TT = (((0,), (1,)), ((), ()))


def dot(left, right, dims=(((1,), (0,)), ((), ()))):
    return lax.dot_general(left, right, dims, preferred_element_type=jnp.float32)


def layer_norm(values, gain):
    centred = values - jnp.mean(values, axis=-1, keepdims=True)
    spread = jnp.mean(centred * centred, axis=-1, keepdims=True)
    return (centred * lax.rsqrt(spread + EPSILON) * gain).astype(jnp.bfloat16)


def unit_columns(fields):
    heads = fields.reshape(HEADS, HEAD_DIM, fields.shape[1])
    squares = jnp.sum(heads * heads, axis=1, keepdims=True)
    return (heads * lax.rsqrt(squares + EPSILON)).reshape(fields.shape)


def project(normed, proj_ref, fields_ref):
    for part in range(3):
        cut = slice(part * WIDTH, (part + 1) * WIDTH)
        fields = dot(proj_ref[:, cut], normed, TT)
        if part < 2:
            fields = unit_columns(fields)
        fields_ref[cut] = fields.astype(jnp.bfloat16)


def hold(held, values):
    for part in range(held.shape[0]):
        held[part] = values[:, part * LANES : (part + 1) * LANES].astype(jnp.float32)


def pick(held, start, count, step):
    return jnp.concatenate(
        [held[part, pl.ds(start, count, stride=step), :] for part in range(held.shape[0])], axis=1
    )


def head_rows(part, head):
    return slice(part * WIDTH + head * HEAD_DIM, part * WIDTH + (head + 1) * HEAD_DIM)


def attend(fields_ref, scale_ref, mixed_ref, scores_ref, weights_ref, totals_ref, span, packed):
    length = span // packed
    owner = lax.broadcasted_iota(jnp.int32, (length, span), 1) // length
    for start in range(0, fields_ref.shape[1], span):
        cut = slice(start, start + span)
        for head in range(HEADS):
            scores_ref[head] = dot(fields_ref[head_rows(1, head), cut], fields_ref[head_rows(0, head), cut], TN)
        for head in range(HEADS):
            factor = scale_ref[head : head + 1]
            for low in range(0, span, LANES):
                lanes = slice(low, low + LANES)
                mine = owner[:, lanes]
                items = range(low // length, (low + LANES - 1) // length + 1) if packed > 1 else range(1)
                scores = scores_ref[head, items[0] * length : (items[0] + 1) * length, lanes]
                for item in items[1:]:
                    scores = jnp.where(mine == item, scores_ref[head, item * length : (item + 1) * length, lanes], scores)
                powers = jnp.exp2((scores - jnp.max(scores, axis=0, keepdims=True)) * factor)
                totals_ref[head, :, lanes] = 1.0 / jnp.sum(powers, axis=0, keepdims=True)
                for item in range(packed):
                    part = powers if packed == 1 else jnp.where(mine == item, powers, 0.0)
                    weights_ref[head, item * length : (item + 1) * length, lanes] = part.astype(jnp.bfloat16)
        for head in range(HEADS):
            mixed = dot(fields_ref[head_rows(2, head), cut], weights_ref[head]) * totals_ref[head]
            mixed_ref[head_rows(0, head), cut] = mixed.astype(jnp.bfloat16)


def pack_kernel(tokens_ref, *refs):
    pieces, held = refs[:-1], refs[-1]
    frames, patches = tokens_ref.shape[0], tokens_ref.shape[1] // len(pieces)
    me = lax.axis_index("tm")
    for frame in range(frames):
        for part in range(held.shape[0]):
            held[part, frame] = tokens_ref[frame, :, part * LANES : (part + 1) * LANES].astype(jnp.float32)
    for index, piece in enumerate(pieces):
        start = pl.multiple_of((me ^ index) * patches, patches)
        for part in range(held.shape[0]):
            rows = [held[part, frame, pl.ds(start, patches)] for frame in range(frames)]
            piece[:, part * LANES : (part + 1) * LANES] = jnp.concatenate(rows, axis=0).astype(jnp.bfloat16)


def time_kernel(frames, count, scale_ref, gain_ref, proj_ref, out_ref, *refs):
    pieces, (stream_ref, held, result, fields, mixed, *work) = refs[:count], refs[count:]
    patches = stream_ref.shape[0] // frames
    span, packed = time_span(frames, patches)
    me = lax.axis_index("tm")
    for index, piece in enumerate(pieces):
        size = piece.shape[0]
        start = 0 if count == 1 else pl.multiple_of((me ^ index) * size, size)
        for part in range(held.shape[0]):
            held[part, pl.ds(start, size)] = piece[:, part * LANES : (part + 1) * LANES].astype(jnp.float32)
    tokens = jnp.concatenate([pick(held, patch, frames, patches) for patch in range(patches)], axis=0)
    project(layer_norm(tokens, gain_ref[...]), proj_ref, fields)
    attend(fields, scale_ref, mixed, *work, span, packed)
    update = dot(mixed[...], out_ref[...], TN)
    for patch in range(patches):
        stream = pick(held, patch, frames, patches) + update[patch * frames : (patch + 1) * frames]
        for part in range(result.shape[0]):
            result[part, pl.ds(patch, frames, stride=patches), :] = stream[:, part * LANES : (part + 1) * LANES]
    for part in range(result.shape[0]):
        stream_ref[:, part * LANES : (part + 1) * LANES] = result[part].astype(jnp.bfloat16)


def space_kernel(senders, sides, scale_ref, gain_ref, proj_ref, out_ref, stream_ref, *refs):
    pieces, (block, held, fields, mixed, *work) = refs[:sides], refs[sides:]
    frames, side_patches = pieces[0].shape[:2]
    piece = stream_ref.shape[0] // senders // frames
    hold(held, stream_ref)

    def ordered():
        parts = []
        for frame in range(frames):
            for side in range(sides):
                if piece % 8:
                    start = (side * frames + frame) * piece
                    parts.append(pick(held, start, senders // sides, sides * frames))
                else:
                    for sender in range(side, senders, sides):
                        parts.append(pick(held, (sender * frames + frame) * piece, piece, 1))
        return jnp.concatenate(parts, axis=0)

    project(layer_norm(ordered(), gain_ref[...]), proj_ref, fields)
    attend(fields, scale_ref, mixed, *work, sides * side_patches, 1)
    stream = ordered() + dot(mixed[...], out_ref[...], TN)
    for frame in range(frames):
        for side in range(sides):
            start = (frame * sides + side) * side_patches
            block[side, frame] = stream[start : start + side_patches].astype(jnp.bfloat16)
    me = lax.axis_index("patch")
    for index in range(sides):
        pieces[index][...] = block[me ^ index]


def place_kernel(*refs):
    count = len(refs) // 2
    pieces, whole, sems = refs[:count], refs[count], refs[count + 1 :]
    frames = pieces[0].shape[0]
    me = lax.axis_index("patch")
    copies = [
        pltpu.make_async_copy(piece, whole.at[pl.ds((me ^ index) * frames, frames)], sems[index])
        for index, piece in enumerate(pieces)
    ]
    for copy in copies:
        copy.start()
    for copy in copies:
        copy.wait()


def time_span(frames, patches):
    packed = max(1, min(patches, LANES // frames))
    return packed * frames, packed


def work_space(rows, span):
    return [
        pltpu.VMEM((3 * WIDTH, rows), jnp.bfloat16),
        pltpu.VMEM((WIDTH, rows), jnp.bfloat16),
        pltpu.VMEM((HEADS, span, span), jnp.float32),
        pltpu.VMEM((HEADS, span, span), jnp.bfloat16),
        pltpu.VMEM((HEADS, 1, span), jnp.float32),
    ]


def small_kernel(*refs):
    count = len(refs) // 2
    for source, target in zip(refs[:count], refs[count:]):
        target[...] = jnp.broadcast_to(source[...], target.shape) * (LOG2_E if target.shape[0] == HEADS else 1.0)


def small(time_scale, space_scale, time_gain, space_gain):
    whole = pl.BlockSpec(memory_space=pltpu.VMEM)
    shapes = [(HEADS, LANES), (HEADS, LANES), (1, WIDTH), (1, WIDTH)]
    return pl.pallas_call(
        small_kernel,
        out_shape=[jax.ShapeDtypeStruct(shape, jnp.float32) for shape in shapes],
        in_specs=[whole] * 4,
        out_specs=[whole] * 4,
        compiler_params=pltpu.CompilerParams(vmem_limit_bytes=1024 * 1024),
        cost_estimate=pl.CostEstimate(flops=10**10, bytes_accessed=10**5, transcendentals=0),
    )(time_scale[:, None], space_scale[:, None], time_gain[None], space_gain[None])


def call(kernel, out_shapes, scratch, scale, gain, proj, out, *rows):
    whole = pl.BlockSpec(memory_space=pltpu.VMEM)
    return pl.pallas_call(
        kernel,
        out_shape=[jax.ShapeDtypeStruct(shape, jnp.bfloat16) for shape in out_shapes],
        in_specs=[whole] * (4 + len(rows)),
        out_specs=[whole] * len(out_shapes),
        scratch_shapes=scratch,
        compiler_params=pltpu.CompilerParams(vmem_limit_bytes=VMEM_BYTES),
        cost_estimate=pl.CostEstimate(flops=10**10, bytes_accessed=7 * 10**6, transcendentals=10**6),
    )(scale, gain, proj, out, *rows)


def pack(tokens, peers):
    frames, patches, width = tokens.shape
    whole = pl.BlockSpec(memory_space=pltpu.VMEM)
    return pl.pallas_call(
        pack_kernel,
        out_shape=[jax.ShapeDtypeStruct((frames * patches // peers, width), tokens.dtype)] * peers,
        in_specs=[whole],
        out_specs=[whole] * peers,
        scratch_shapes=[pltpu.VMEM((width // LANES, frames, patches, LANES), jnp.float32)],
        compiler_params=pltpu.CompilerParams(vmem_limit_bytes=8 * 1024 * 1024),
    )(tokens)


def place(pieces):
    anywhere = pl.BlockSpec(memory_space=pl.ANY)
    frames, patches, width = pieces[0].shape
    return pl.pallas_call(
        place_kernel,
        out_shape=jax.ShapeDtypeStruct((frames * len(pieces), patches, width), pieces[0].dtype),
        in_specs=[anywhere] * len(pieces),
        out_specs=anywhere,
        scratch_shapes=[pltpu.SemaphoreType.DMA] * len(pieces),
        compiler_params=pltpu.CompilerParams(vmem_limit_bytes=1024 * 1024),
    )(*pieces)


def swap(pieces, axis):
    size = len(pieces)
    return [
        lax.ppermute(piece, axis, [(i, i ^ index) for i in range(size)]) if index else piece
        for index, piece in enumerate(pieces)
    ]


def per_device(
    tokens,
    time_gain,
    time_proj,
    time_out,
    time_scale,
    space_gain,
    space_proj,
    space_out,
    space_scale,
):
    frames, local_count, width = tokens.shape
    peers, sides = lax.axis_size("tm"), lax.axis_size("patch")
    rows = frames * local_count
    all_frames = frames * peers
    time_scale, space_scale, time_gain, space_gain = small(time_scale, space_scale, time_gain, space_gain)
    if peers <= 8:
        arrived = swap(pack(tokens, peers), "tm")
    else:
        outgoing = tokens.reshape(frames, peers, local_count // peers, width)
        outgoing = jnp.swapaxes(outgoing, 0, 1).reshape(peers, rows // peers, width)
        arrived = [lax.all_to_all(outgoing, "tm", split_axis=0, concat_axis=0, tiled=True).reshape(rows, width)]
    held = pltpu.VMEM((width // LANES, rows, LANES), jnp.float32)
    stream = call(
        functools.partial(time_kernel, all_frames, len(arrived)),
        [(rows, width)],
        [held, held] + work_space(rows, time_span(all_frames, local_count // peers)[0]),
        time_scale, time_gain, time_proj, time_out, *arrived,
    )[0]
    senders = peers * sides
    stream = lax.all_to_all(
        stream.reshape(senders, rows // senders, width), ("tm", "patch"), split_axis=0, concat_axis=0, tiled=True
    ).reshape(rows, width)
    piece = (frames // sides, local_count, width)
    blocks = call(
        functools.partial(space_kernel, senders, sides),
        [piece] * sides,
        [pltpu.VMEM((sides,) + piece, jnp.bfloat16), held] + work_space(rows, sides * local_count),
        space_scale, space_gain, space_proj, space_out, stream,
    )
    return place(swap(blocks, "patch"))


def solution(mesh):
    in_specs = (P("tm", "patch", None), P(), P(), P(), P(), P(), P(), P(), P())
    out_specs = P("tm", "patch", None)
    return jax.shard_map(
        per_device, mesh=mesh, in_specs=in_specs, out_specs=out_specs, check_vma=False
    )
```

```python
import functools
import math

import jax
import jax.numpy as jnp
from jax import lax
from jax.experimental import pallas as pl
from jax.experimental.pallas import tpu as pltpu
from jax.sharding import PartitionSpec as P

HEADS = 12
HEAD_DIM = 64
WIDTH = HEADS * HEAD_DIM
EPSILON = 1e-06
LOG2_E = math.log2(math.e)
LANES = 128
VMEM_BYTES = 24 * 1024 * 1024

TN = (((0,), (0,)), ((), ()))
TT = (((0,), (1,)), ((), ()))


def dot(left, right, dims=(((1,), (0,)), ((), ()))):
    return lax.dot_general(left, right, dims, preferred_element_type=jnp.float32)


def layer_norm(values, gain):
    centred = values - jnp.mean(values, axis=-1, keepdims=True)
    spread = jnp.mean(centred * centred, axis=-1, keepdims=True)
    return (centred * lax.rsqrt(spread + EPSILON) * gain).astype(jnp.bfloat16)


def unit_columns(fields):
    heads = fields.reshape(HEADS, HEAD_DIM, fields.shape[1])
    squares = jnp.sum(heads * heads, axis=1, keepdims=True)
    return (heads * lax.rsqrt(squares + EPSILON)).reshape(fields.shape)


def project(normed, proj_ref, fields_ref):
    for part in range(3):
        cut = slice(part * WIDTH, (part + 1) * WIDTH)
        fields = dot(proj_ref[:, cut], normed, TT)
        if part < 2:
            fields = unit_columns(fields)
        fields_ref[cut] = fields.astype(jnp.bfloat16)


def hold(held, values):
    for part in range(held.shape[0]):
        held[part] = values[:, part * LANES : (part + 1) * LANES].astype(jnp.float32)


def pick(held, start, count, step):
    return jnp.concatenate(
        [held[part, pl.ds(start, count, stride=step), :] for part in range(held.shape[0])], axis=1
    )


def head_rows(part, head):
    return slice(part * WIDTH + head * HEAD_DIM, part * WIDTH + (head + 1) * HEAD_DIM)


def attend(fields_ref, scale_ref, mixed_ref, scores_ref, weights_ref, totals_ref, span, packed):
    length = span // packed
    owner = lax.broadcasted_iota(jnp.int32, (length, span), 1) // length
    for start in range(0, fields_ref.shape[1], span):
        cut = slice(start, start + span)
        for head in range(HEADS):
            scores_ref[head] = dot(fields_ref[head_rows(1, head), cut], fields_ref[head_rows(0, head), cut], TN)
        for head in range(HEADS):
            factor = scale_ref[head : head + 1]
            for low in range(0, span, LANES):
                lanes = slice(low, low + LANES)
                mine = owner[:, lanes]
                items = range(low // length, (low + LANES - 1) // length + 1) if packed > 1 else range(1)
                scores = scores_ref[head, items[0] * length : (items[0] + 1) * length, lanes]
                for item in items[1:]:
                    scores = jnp.where(mine == item, scores_ref[head, item * length : (item + 1) * length, lanes], scores)
                powers = jnp.exp2((scores - jnp.max(scores, axis=0, keepdims=True)) * factor)
                totals_ref[head, :, lanes] = 1.0 / jnp.sum(powers, axis=0, keepdims=True)
                for item in range(packed):
                    part = powers if packed == 1 else jnp.where(mine == item, powers, 0.0)
                    weights_ref[head, item * length : (item + 1) * length, lanes] = part.astype(jnp.bfloat16)
        for head in range(HEADS):
            mixed = dot(fields_ref[head_rows(2, head), cut], weights_ref[head]) * totals_ref[head]
            mixed_ref[head_rows(0, head), cut] = mixed.astype(jnp.bfloat16)


ORDER = {2: [1], 4: [2, 3, 1], 8: [2, 4, 6, 5, 7, 3, 1]}


def pack_kernel(tokens_ref, *refs):
    pieces, held = refs[:-1], refs[-1]
    frames, patches = tokens_ref.shape[0], tokens_ref.shape[1] // len(pieces)
    me = lax.axis_index("tm")
    for frame in range(frames):
        for part in range(held.shape[0]):
            held[part, frame] = tokens_ref[frame, :, part * LANES : (part + 1) * LANES].astype(jnp.float32)
    for index, piece in enumerate(pieces):
        start = pl.multiple_of((me ^ index) * patches, patches)
        for part in range(held.shape[0]):
            rows = [held[part, frame, pl.ds(start, patches)] for frame in range(frames)]
            piece[:, part * LANES : (part + 1) * LANES] = jnp.concatenate(rows, axis=0).astype(jnp.bfloat16)


def time_kernel(frames, count, scale_ref, gain_ref, proj_ref, out_ref, *refs):
    pieces, (stream_ref, held, result, fields, mixed, *work) = refs[:count], refs[count:]
    order = [0] + ORDER[count] if count > 1 else [0]
    patches = stream_ref.shape[0] // frames
    span, packed = time_span(frames, patches)
    me = lax.axis_index("tm")
    for index, piece in zip(order, pieces):
        size = piece.shape[0]
        start = 0 if count == 1 else pl.multiple_of((me ^ index) * size, size)
        for part in range(held.shape[0]):
            held[part, pl.ds(start, size)] = piece[:, part * LANES : (part + 1) * LANES].astype(jnp.float32)
    tokens = jnp.concatenate([pick(held, patch, frames, patches) for patch in range(patches)], axis=0)
    project(layer_norm(tokens, gain_ref[...]), proj_ref, fields)
    attend(fields, scale_ref, mixed, *work, span, packed)
    update = dot(mixed[...], out_ref[...], TN)
    for patch in range(patches):
        stream = pick(held, patch, frames, patches) + update[patch * frames : (patch + 1) * frames]
        for part in range(result.shape[0]):
            result[part, pl.ds(patch, frames, stride=patches), :] = stream[:, part * LANES : (part + 1) * LANES]
    for part in range(result.shape[0]):
        stream_ref[:, part * LANES : (part + 1) * LANES] = result[part].astype(jnp.bfloat16)


def space_kernel(
    frame, senders, sides, frames, scale_ref, gain_ref, proj_ref, out_ref, stream_ref, *refs
):
    pieces, (block, held, fields, mixed, *work) = refs[:sides], refs[sides:]
    side_patches = pieces[0].shape[0]
    piece = stream_ref.shape[0] // senders // frames
    hold(held, stream_ref)

    def ordered():
        parts = []
        for side in range(sides):
            if piece % 8:
                start = (side * frames + frame) * piece
                parts.append(pick(held, start, senders // sides, sides * frames))
            else:
                for sender in range(side, senders, sides):
                    parts.append(pick(held, (sender * frames + frame) * piece, piece, 1))
        return jnp.concatenate(parts, axis=0)

    project(layer_norm(ordered(), gain_ref[...]), proj_ref, fields)
    attend(fields, scale_ref, mixed, *work, sides * side_patches, 1)
    stream = ordered() + dot(mixed[...], out_ref[...], TN)
    for side in range(sides):
        block[side] = stream[side * side_patches : (side + 1) * side_patches].astype(jnp.bfloat16)
    me = lax.axis_index("patch")
    for index in range(sides):
        pieces[index][...] = block[me ^ index]


def place_kernel(frame, frames, sides, *refs):
    pieces, whole, sems = refs[:sides], refs[-sides - 1], refs[-sides:]
    me = lax.axis_index("patch")
    copies = [
        pltpu.make_async_copy(piece, whole.at[(me ^ index) * frames + frame], sems[index])
        for index, piece in enumerate(pieces)
    ]
    for copy in copies:
        copy.start()
    for copy in copies:
        copy.wait()


def time_span(frames, patches):
    packed = max(1, min(patches, LANES // frames))
    return packed * frames, packed


def work_space(rows, span):
    return [
        pltpu.VMEM((3 * WIDTH, rows), jnp.bfloat16),
        pltpu.VMEM((WIDTH, rows), jnp.bfloat16),
        pltpu.VMEM((HEADS, span, span), jnp.float32),
        pltpu.VMEM((HEADS, span, span), jnp.bfloat16),
        pltpu.VMEM((HEADS, 1, span), jnp.float32),
    ]


def small_kernel(*refs):
    count = len(refs) // 2
    for source, target in zip(refs[:count], refs[count:]):
        target[...] = jnp.broadcast_to(source[...], target.shape) * (LOG2_E if target.shape[0] == HEADS else 1.0)


def small(time_scale, space_scale, time_gain, space_gain):
    whole = pl.BlockSpec(memory_space=pltpu.VMEM)
    shapes = [(HEADS, LANES), (HEADS, LANES), (1, WIDTH), (1, WIDTH)]
    return pl.pallas_call(
        small_kernel,
        out_shape=[jax.ShapeDtypeStruct(shape, jnp.float32) for shape in shapes],
        in_specs=[whole] * 4,
        out_specs=[whole] * 4,
        compiler_params=pltpu.CompilerParams(vmem_limit_bytes=1024 * 1024),
        cost_estimate=pl.CostEstimate(flops=10**10, bytes_accessed=10**5, transcendentals=0),
    )(time_scale[:, None], space_scale[:, None], time_gain[None], space_gain[None])


def call(kernel, out_shapes, scratch, scale, gain, proj, out, *rows):
    whole = pl.BlockSpec(memory_space=pltpu.VMEM)
    return pl.pallas_call(
        kernel,
        out_shape=[jax.ShapeDtypeStruct(shape, jnp.bfloat16) for shape in out_shapes],
        in_specs=[whole] * (4 + len(rows)),
        out_specs=[whole] * len(out_shapes),
        scratch_shapes=scratch,
        compiler_params=pltpu.CompilerParams(vmem_limit_bytes=VMEM_BYTES),
        cost_estimate=pl.CostEstimate(flops=10**10, bytes_accessed=7 * 10**6, transcendentals=10**6),
    )(scale, gain, proj, out, *rows)


def pack(tokens, peers):
    frames, patches, width = tokens.shape
    whole = pl.BlockSpec(memory_space=pltpu.VMEM)
    return pl.pallas_call(
        pack_kernel,
        out_shape=[jax.ShapeDtypeStruct((frames * patches // peers, width), tokens.dtype)] * peers,
        in_specs=[whole],
        out_specs=[whole] * peers,
        scratch_shapes=[pltpu.VMEM((width // LANES, frames, patches, LANES), jnp.float32)],
        compiler_params=pltpu.CompilerParams(vmem_limit_bytes=8 * 1024 * 1024),
    )(tokens)


def place(frame, frames, pieces, whole):
    anywhere = pl.BlockSpec(memory_space=pl.ANY)
    sides = len(pieces)
    others = [] if whole is None else [whole]
    return pl.pallas_call(
        functools.partial(place_kernel, frame, frames, sides),
        out_shape=jax.ShapeDtypeStruct((sides * frames,) + pieces[0].shape, pieces[0].dtype),
        in_specs=[anywhere] * (sides + len(others)),
        out_specs=anywhere,
        scratch_shapes=[pltpu.SemaphoreType.DMA] * sides,
        input_output_aliases={sides: 0} if others else {},
        compiler_params=pltpu.CompilerParams(vmem_limit_bytes=1024 * 1024),
        cost_estimate=pl.CostEstimate(flops=10**10, bytes_accessed=10**6, transcendentals=0),
    )(*pieces, *others)


def swap(pieces, axis):
    size = len(pieces)
    arrived = list(pieces)
    for index in ORDER[size]:
        arrived[index] = lax.ppermute(pieces[index], axis, [(i, i ^ index) for i in range(size)])
    return arrived


def per_device(
    tokens,
    time_gain,
    time_proj,
    time_out,
    time_scale,
    space_gain,
    space_proj,
    space_out,
    space_scale,
):
    frames, local_count, width = tokens.shape
    peers, sides = lax.axis_size("tm"), lax.axis_size("patch")
    rows = frames * local_count
    all_frames = frames * peers
    time_scale, space_scale, time_gain, space_gain = small(time_scale, space_scale, time_gain, space_gain)
    if peers <= 8:
        arrived = swap(pack(tokens, peers), "tm")
        arrived = [arrived[index] for index in [0] + ORDER[peers]]
    else:
        outgoing = tokens.reshape(frames, peers, local_count // peers, width)
        outgoing = jnp.swapaxes(outgoing, 0, 1).reshape(peers, rows // peers, width)
        arrived = [lax.all_to_all(outgoing, "tm", split_axis=0, concat_axis=0, tiled=True).reshape(rows, width)]
    held = pltpu.VMEM((width // LANES, rows, LANES), jnp.float32)
    stream = call(
        functools.partial(time_kernel, all_frames, len(arrived)),
        [(rows, width)],
        [held, held] + work_space(rows, time_span(all_frames, local_count // peers)[0]),
        time_scale, time_gain, time_proj, time_out, *arrived,
    )[0]
    senders = peers * sides
    stream = lax.all_to_all(
        stream.reshape(senders, rows // senders, width), ("tm", "patch"), split_axis=0, concat_axis=0, tiled=True
    ).reshape(rows, width)
    own_frames = frames // sides
    piece = (local_count, width)
    block = None
    for frame in range(own_frames):
        blocks = call(
            functools.partial(space_kernel, frame, senders, sides, own_frames),
            [piece] * sides,
            [pltpu.VMEM((sides,) + piece, jnp.bfloat16), held] + work_space(rows // own_frames, sides * local_count),
            space_scale, space_gain, space_proj, space_out, stream,
        )
        block = place(frame, own_frames, swap(blocks, "patch"), block)
    return block


def solution(mesh):
    in_specs = (P("tm", "patch", None), P(), P(), P(), P(), P(), P(), P(), P())
    out_specs = P("tm", "patch", None)
    return jax.shard_map(
        per_device, mesh=mesh, in_specs=in_specs, out_specs=out_specs, check_vma=False
    )
```

```python
import functools
import math

import jax
import jax.numpy as jnp
from jax import lax
from jax.experimental import pallas as pl
from jax.experimental.pallas import tpu as pltpu
from jax.sharding import PartitionSpec as P

HEADS = 12
HEAD_DIM = 64
WIDTH = HEADS * HEAD_DIM
EPSILON = 1e-06
LOG2_E = math.log2(math.e)
LANES = 128
AHEAD = 12
VMEM_BYTES = 24 * 1024 * 1024

TN = (((0,), (0,)), ((), ()))
TT = (((0,), (1,)), ((), ()))


def dot(left, right, dims=(((1,), (0,)), ((), ()))):
    return lax.dot_general(left, right, dims, preferred_element_type=jnp.float32)


def layer_norm(values, gain):
    centred = values - jnp.mean(values, axis=-1, keepdims=True)
    spread = jnp.mean(centred * centred, axis=-1, keepdims=True)
    return (centred * lax.rsqrt(spread + EPSILON) * gain).astype(jnp.bfloat16)


def unit_columns(fields):
    heads = fields.reshape(HEADS, HEAD_DIM, fields.shape[1])
    squares = jnp.sum(heads * heads, axis=1, keepdims=True)
    return (heads * lax.rsqrt(squares + EPSILON)).reshape(fields.shape)


def project(normed, proj_ref, fields_ref):
    for part in range(3):
        cut = slice(part * WIDTH, (part + 1) * WIDTH)
        fields = dot(proj_ref[:, cut], normed, TT)
        if part < 2:
            fields = unit_columns(fields)
        fields_ref[cut] = fields.astype(jnp.bfloat16)


def hold(held, values):
    for part in range(held.shape[0]):
        held[part] = values[:, part * LANES : (part + 1) * LANES].astype(jnp.float32)


def pick(held, start, count, step):
    return jnp.concatenate(
        [held[part, pl.ds(start, count, stride=step), :] for part in range(held.shape[0])], axis=1
    )


def head_rows(part, head):
    return slice(part * WIDTH + head * HEAD_DIM, part * WIDTH + (head + 1) * HEAD_DIM)


def attend(fields_ref, scale_ref, mixed_ref, scores_ref, weights_ref, totals_ref, groups, packed, length):
    span = groups * packed * length
    runs = fields_ref.shape[1] // span
    item_of = (lax.broadcasted_iota(jnp.int32, (1, span), 1) // length) % packed

    def rows(group, item):
        first = (group * packed + item) * length
        return slice(first, first + length)

    def score(at, head):
        cut = slice(at // HEADS * span, (at // HEADS + 1) * span)
        scores_ref[at] = dot(fields_ref[head_rows(1, head), cut], fields_ref[head_rows(0, head), cut], TN)

    def soften(at, head):
        factor = scale_ref[head : head + 1]
        for low in range(0, span, LANES):
            lanes = slice(low, low + LANES)
            mine = jnp.broadcast_to(item_of[:, lanes], (length, LANES))
            scores = []
            for group in range(groups):
                own = scores_ref[at, rows(group, 0), lanes]
                for item in range(1, packed):
                    own = jnp.where(mine == item, scores_ref[at, rows(group, item), lanes], own)
                scores.append(own)
            largest = functools.reduce(jnp.maximum, [jnp.max(own, axis=0, keepdims=True) for own in scores])
            powers = [jnp.exp2((own - largest) * factor) for own in scores]
            totals_ref[at, :, lanes] = 1.0 / sum(jnp.sum(part, axis=0, keepdims=True) for part in powers)
            for group in range(groups):
                for item in range(packed):
                    part = powers[group] if packed == 1 else jnp.where(mine == item, powers[group], 0.0)
                    weights_ref[at, rows(group, item), lanes] = part.astype(jnp.bfloat16)

    def mix(at, head):
        cut = slice(at // HEADS * span, (at // HEADS + 1) * span)
        mixed = dot(fields_ref[head_rows(2, head), cut], weights_ref[at]) * totals_ref[at]
        mixed_ref[head_rows(0, head), cut] = mixed.astype(jnp.bfloat16)

    count = runs * HEADS
    apart = max(1, AHEAD * 256 // span)
    for step in range(count + 2 * apart):
        for stage, late in ((score, 0), (soften, apart), (mix, 2 * apart)):
            at = step - late
            if 0 <= at < count:
                stage(at, at % HEADS)


GROUPS = [[0, 2, 4, 6], [5, 7, 3, 1]]
ORDER = {2: [1], 4: [2, 3, 1], 8: [2, 4, 6, 5, 7, 3, 1]}


def pack_kernel(tokens_ref, *refs):
    pieces, held = refs[:-1], refs[-1]
    frames, patches = tokens_ref.shape[0], tokens_ref.shape[1] // len(pieces)
    me = lax.axis_index("tm")
    for frame in range(frames):
        for part in range(held.shape[0]):
            held[part, frame] = tokens_ref[frame, :, part * LANES : (part + 1) * LANES].astype(jnp.float32)
    for index, piece in enumerate(pieces):
        start = pl.multiple_of((me ^ index) * patches, patches)
        for part in range(held.shape[0]):
            rows = [held[part, frame, pl.ds(start, patches)] for frame in range(frames)]
            piece[:, part * LANES : (part + 1) * LANES] = jnp.concatenate(rows, axis=0).astype(jnp.bfloat16)


def hold_pieces(held, pieces):
    start = 0
    for piece in pieces:
        for part in range(held.shape[0]):
            held[part, start : start + piece.shape[0]] = piece[:, part * LANES : (part + 1) * LANES].astype(jnp.float32)
        start += piece.shape[0]


def fields_kernel(patches, gain_ref, proj_ref, *refs):
    pieces, (fields_ref, held) = refs[:-2], refs[-2:]
    hold_pieces(held, pieces)
    tokens = [pick(held, patch, held.shape[1] // patches, patches) for patch in range(patches)]
    project(layer_norm(jnp.concatenate(tokens, axis=0), gain_ref[...]), proj_ref, fields_ref)


def time_kernel(groups, patches, scale_ref, gain_ref, proj_ref, out_ref, *refs):
    count, ready = sum(map(len, groups)), len(groups) - 1
    fields, pieces = refs[:ready], refs[ready : ready + count]
    stream_ref, held, result, merged, mixed, own_fields, *work = refs[ready + count :]
    fields = fields + (own_fields,)
    rows = held.shape[1] // len(groups)
    length = rows // patches
    packed = time_packed(len(groups) * length, patches)
    hold_pieces(held, pieces)
    turn = len(groups) == 2
    order = [patch ^ packed if turn else patch for patch in range(patches)]
    tokens = [pick(held, ready * rows + patch, length, patches) for patch in order]
    project(layer_norm(jnp.concatenate(tokens, axis=0), gain_ref[...]), proj_ref, own_fields)
    if turn:
        near = lax.broadcasted_iota(jnp.int32, (HEAD_DIM, LANES), 1) < packed * length
        for low in range(0, 3 * WIDTH, HEAD_DIM):
            cut = slice(low, low + HEAD_DIM)
            for tile in range(0, rows, LANES):
                first, second = (group[cut, tile : tile + LANES] for group in fields)
                merged[cut, 2 * tile : 2 * tile + LANES] = jnp.where(near, first, second)
                merged[cut, 2 * tile + LANES : 2 * tile + 2 * LANES] = jnp.where(near, second, first)
    else:
        merged = own_fields
    attend(merged, scale_ref, mixed, *work, len(groups), packed, length)
    half = max(patches // 2, packed)
    for patch in range(patches):
        if patch % half == 0:
            cut = slice(patch * len(groups) * length, (patch + half) * len(groups) * length)
            update = dot(mixed[:, cut], out_ref[...], TN)
        for group in range(len(groups)):
            unit = patch % half // packed
            slot = group ^ (unit % 2) if turn else group
            first = ((unit * len(groups) + slot) * packed + patch % packed) * length
            place = pl.ds(group * rows + patch, length, stride=patches)
            for part in range(result.shape[0]):
                lanes = slice(part * LANES, (part + 1) * LANES)
                result[part, place, :] = held[part, place, :] + update[first : first + length, lanes]
    me = lax.axis_index("tm")
    size = pieces[0].shape[0]
    for index, piece in enumerate(place for group in groups for place in group):
        start = 0 if count == 1 else pl.multiple_of((me ^ piece) * size, size)
        for part in range(result.shape[0]):
            values = result[part, index * size : (index + 1) * size]
            stream_ref[pl.ds(start, size), part * LANES : (part + 1) * LANES] = values.astype(jnp.bfloat16)


def space_kernel(
    frame, senders, sides, frames, scale_ref, gain_ref, proj_ref, out_ref, stream_ref, *refs
):
    pieces, (block, held, tokens, fields, mixed, *work) = refs[:sides], refs[sides:]
    side_patches = pieces[0].shape[0]
    piece = stream_ref.shape[0] // senders // frames
    if piece % 8:
        hold(held, stream_ref)
        for side in range(sides):
            rows = pick(held, (side * frames + frame) * piece, senders // sides, sides * frames)
            tokens[side * side_patches : (side + 1) * side_patches] = rows
    else:
        for sender in range(senders):
            block_rows = stream_ref[sender * frames * piece : (sender + 1) * frames * piece].astype(jnp.float32)
            place = sender % sides * side_patches + sender // sides * piece
            tokens[place : place + piece] = block_rows[frame * piece : (frame + 1) * piece]
    project(layer_norm(tokens[...], gain_ref[...]), proj_ref, fields)
    attend(fields, scale_ref, mixed, *work, 1, 1, sides * side_patches)
    stream = tokens[...] + dot(mixed[...], out_ref[...], TN)
    for side in range(sides):
        block[side] = stream[side * side_patches : (side + 1) * side_patches].astype(jnp.bfloat16)
    me = lax.axis_index("patch")
    for index in range(sides):
        pieces[index][...] = block[me ^ index]


def place_kernel(frame, frames, sides, *refs):
    pieces, whole, sems = refs[:sides], refs[-sides - 1], refs[-sides:]
    me = lax.axis_index("patch")
    copies = [
        pltpu.make_async_copy(piece, whole.at[(me ^ index) * frames + frame], sems[index])
        for index, piece in enumerate(pieces)
    ]
    for copy in copies:
        copy.start()
    for copy in copies:
        copy.wait()


def time_packed(frames, patches):
    return max(1, min(patches, LANES // frames))


def work_space(rows, span):
    return [
        pltpu.VMEM((3 * WIDTH, rows), jnp.bfloat16),
        pltpu.VMEM((WIDTH, rows), jnp.bfloat16),
    ], [
        pltpu.VMEM((rows // span * HEADS, span, span), jnp.float32),
        pltpu.VMEM((rows // span * HEADS, span, span), jnp.bfloat16),
        pltpu.VMEM((rows // span * HEADS, 1, span), jnp.float32),
    ]


def small_kernel(packed_ref, time_scale_ref, space_scale_ref, time_gain_ref, space_gain_ref):
    time_gain_ref[...] = packed_ref[:, :WIDTH]
    space_gain_ref[...] = packed_ref[:, WIDTH : 2 * WIDTH]
    for index, target in enumerate((time_scale_ref, space_scale_ref)):
        for head in range(HEADS):
            place = 2 * WIDTH + index * HEADS + head
            target[head : head + 1] = jnp.broadcast_to(packed_ref[:, place : place + 1] * LOG2_E, (1, LANES))


def small(time_scale, space_scale, time_gain, space_gain):
    whole = pl.BlockSpec(memory_space=pltpu.VMEM)
    shapes = [(HEADS, LANES), (HEADS, LANES), (1, WIDTH), (1, WIDTH)]
    return pl.pallas_call(
        small_kernel,
        out_shape=[jax.ShapeDtypeStruct(shape, jnp.float32) for shape in shapes],
        in_specs=[whole],
        out_specs=[whole] * 4,
        compiler_params=pltpu.CompilerParams(vmem_limit_bytes=1024 * 1024),
        cost_estimate=pl.CostEstimate(flops=10**10, bytes_accessed=10**5, transcendentals=0),
    )(jnp.concatenate([time_gain, space_gain, time_scale, space_scale])[None])


def call(kernel, out_shapes, scratch, scale, gain, proj, out, *rows):
    whole = pl.BlockSpec(memory_space=pltpu.VMEM)
    return pl.pallas_call(
        kernel,
        out_shape=[jax.ShapeDtypeStruct(shape, jnp.bfloat16) for shape in out_shapes],
        in_specs=[whole] * (4 + len(rows)),
        out_specs=[whole] * len(out_shapes),
        scratch_shapes=scratch,
        compiler_params=pltpu.CompilerParams(vmem_limit_bytes=VMEM_BYTES),
        cost_estimate=pl.CostEstimate(flops=10**10, bytes_accessed=7 * 10**6, transcendentals=10**6),
    )(scale, gain, proj, out, *rows)


def project_early(patches, gain, proj, pieces):
    whole = pl.BlockSpec(memory_space=pltpu.VMEM)
    rows = sum(piece.shape[0] for piece in pieces)
    return pl.pallas_call(
        functools.partial(fields_kernel, patches),
        out_shape=jax.ShapeDtypeStruct((3 * WIDTH, rows), jnp.bfloat16),
        in_specs=[whole] * (2 + len(pieces)),
        out_specs=whole,
        scratch_shapes=[pltpu.VMEM((WIDTH // LANES, rows, LANES), jnp.float32)],
        compiler_params=pltpu.CompilerParams(vmem_limit_bytes=VMEM_BYTES),
        cost_estimate=pl.CostEstimate(flops=5 * 10**9, bytes_accessed=7 * 10**6, transcendentals=10**6),
    )(gain, proj, *pieces)


def pack(tokens, peers):
    frames, patches, width = tokens.shape
    whole = pl.BlockSpec(memory_space=pltpu.VMEM)
    return pl.pallas_call(
        pack_kernel,
        out_shape=[jax.ShapeDtypeStruct((frames * patches // peers, width), tokens.dtype)] * peers,
        in_specs=[whole],
        out_specs=[whole] * peers,
        scratch_shapes=[pltpu.VMEM((width // LANES, frames, patches, LANES), jnp.float32)],
        compiler_params=pltpu.CompilerParams(vmem_limit_bytes=8 * 1024 * 1024),
    )(tokens)


def place(frame, frames, pieces, whole):
    anywhere = pl.BlockSpec(memory_space=pl.ANY)
    sides = len(pieces)
    others = [] if whole is None else [whole]
    return pl.pallas_call(
        functools.partial(place_kernel, frame, frames, sides),
        out_shape=jax.ShapeDtypeStruct((sides * frames,) + pieces[0].shape, pieces[0].dtype),
        in_specs=[anywhere] * (sides + len(others)),
        out_specs=anywhere,
        scratch_shapes=[pltpu.SemaphoreType.DMA] * sides,
        input_output_aliases={sides: 0} if others else {},
        compiler_params=pltpu.CompilerParams(vmem_limit_bytes=1024 * 1024),
        cost_estimate=pl.CostEstimate(flops=10**10, bytes_accessed=10**6, transcendentals=0),
    )(*pieces, *others)


def swap(pieces, axis):
    size = len(pieces)
    arrived = list(pieces)
    for index in ORDER[size]:
        arrived[index] = lax.ppermute(pieces[index], axis, [(i, i ^ index) for i in range(size)])
    return arrived


def per_device(
    tokens,
    time_gain,
    time_proj,
    time_out,
    time_scale,
    space_gain,
    space_proj,
    space_out,
    space_scale,
):
    frames, local_count, width = tokens.shape
    peers, sides = lax.axis_size("tm"), lax.axis_size("patch")
    rows = frames * local_count
    all_frames = frames * peers
    time_scale, space_scale, time_gain, space_gain = small(time_scale, space_scale, time_gain, space_gain)
    patches = local_count // peers
    fields = []
    if peers == 8:
        groups = GROUPS
        arrived = swap(pack(tokens, peers), "tm")
        arrived = [[arrived[index] for index in group] for group in groups]
        fields = [project_early(patches, time_gain, time_proj, pieces) for pieces in arrived[:-1]]
        arrived = sum(arrived, [])
    else:
        groups = [[0]]
        outgoing = jnp.swapaxes(tokens.reshape(frames, peers, patches, width), 0, 1).reshape(peers, rows // peers, width)
        arrived = [lax.all_to_all(outgoing, "tm", split_axis=0, concat_axis=0, tiled=True).reshape(rows, width)]
    held = pltpu.VMEM((width // LANES, rows, LANES), jnp.float32)
    space, work = work_space(rows, time_packed(all_frames, patches) * all_frames)
    stream = call(
        functools.partial(time_kernel, groups, patches),
        [(rows, width)],
        [held, held] + space + [pltpu.VMEM((3 * width, rows // len(groups)), jnp.bfloat16)] + work,
        time_scale, time_gain, time_proj, time_out, *fields, *arrived,
    )[0]
    senders = peers * sides
    stream = lax.all_to_all(
        stream.reshape(senders, rows // senders, width), ("tm", "patch"), split_axis=0, concat_axis=0, tiled=True
    ).reshape(rows, width)
    own_frames = frames // sides
    piece = (local_count, width)
    space, work = work_space(rows // own_frames, sides * local_count)
    tokens_held = pltpu.VMEM((sides * local_count, width), jnp.float32)
    block = None
    for frame in range(own_frames):
        blocks = call(
            functools.partial(space_kernel, frame, senders, sides, own_frames),
            [piece] * sides,
            [pltpu.VMEM((sides,) + piece, jnp.bfloat16), held, tokens_held] + space + work,
            space_scale, space_gain, space_proj, space_out, stream,
        )
        block = place(frame, own_frames, swap(blocks, "patch"), block)
    return block


def solution(mesh):
    in_specs = (P("tm", "patch", None), P(), P(), P(), P(), P(), P(), P(), P())
    out_specs = P("tm", "patch", None)
    return jax.shard_map(
        per_device, mesh=mesh, in_specs=in_specs, out_specs=out_specs, check_vma=False
    )
```

```python
import functools
import math

import jax
import jax.numpy as jnp
from jax import lax
from jax.experimental import pallas as pl
from jax.experimental.pallas import tpu as pltpu
from jax.sharding import PartitionSpec as P

HEADS = 12
HEAD_DIM = 64
WIDTH = HEADS * HEAD_DIM
EPSILON = 1e-06
LOG2_E = math.log2(math.e)
LANES = 128
AHEAD = 12
VMEM_BYTES = 24 * 1024 * 1024

TN = (((0,), (0,)), ((), ()))
TT = (((0,), (1,)), ((), ()))


def dot(left, right, dims=(((1,), (0,)), ((), ()))):
    return lax.dot_general(left, right, dims, preferred_element_type=jnp.float32)


def layer_norm(values, gain):
    centred = values - jnp.mean(values, axis=-1, keepdims=True)
    spread = jnp.mean(centred * centred, axis=-1, keepdims=True)
    return (centred * lax.rsqrt(spread + EPSILON) * gain).astype(jnp.bfloat16)


def unit_columns(fields):
    heads = fields.reshape(HEADS, HEAD_DIM, fields.shape[1])
    squares = jnp.sum(heads * heads, axis=1, keepdims=True)
    return (heads * lax.rsqrt(squares + EPSILON)).reshape(fields.shape)


def project(normed, proj_ref, fields_ref):
    for part in range(3):
        cut = slice(part * WIDTH, (part + 1) * WIDTH)
        fields = dot(proj_ref[:, cut], normed, TT)
        if part < 2:
            fields = unit_columns(fields)
        fields_ref[cut] = fields.astype(jnp.bfloat16)


def hold(held, values):
    for part in range(held.shape[0]):
        held[part] = values[:, part * LANES : (part + 1) * LANES].astype(jnp.float32)


def pick(held, start, count, step):
    return jnp.concatenate(
        [held[part, pl.ds(start, count, stride=step), :] for part in range(held.shape[0])], axis=1
    )


def head_rows(part, head):
    return slice(part * WIDTH + head * HEAD_DIM, part * WIDTH + (head + 1) * HEAD_DIM)


def attend(fields_ref, scale_ref, mixed_ref, scores_ref, weights_ref, totals_ref, groups, packed, length):
    span = groups * packed * length
    runs = fields_ref.shape[1] // span
    item_of = (lax.broadcasted_iota(jnp.int32, (1, span), 1) // length) % packed

    def rows(group, item):
        first = (group * packed + item) * length
        return slice(first, first + length)

    def score(at, head):
        cut = slice(at // HEADS * span, (at // HEADS + 1) * span)
        scores_ref[at] = dot(fields_ref[head_rows(1, head), cut], fields_ref[head_rows(0, head), cut], TN)

    def soften(at, head):
        factor = scale_ref[head : head + 1]
        for low in range(0, span, LANES):
            lanes = slice(low, low + LANES)
            mine = jnp.broadcast_to(item_of[:, lanes], (length, LANES))
            scores = []
            for group in range(groups):
                own = scores_ref[at, rows(group, 0), lanes]
                for item in range(1, packed):
                    own = jnp.where(mine == item, scores_ref[at, rows(group, item), lanes], own)
                scores.append(own)
            largest = functools.reduce(jnp.maximum, [jnp.max(own, axis=0, keepdims=True) for own in scores])
            powers = [jnp.exp2((own - largest) * factor) for own in scores]
            totals_ref[at, :, lanes] = 1.0 / sum(jnp.sum(part, axis=0, keepdims=True) for part in powers)
            for group in range(groups):
                for item in range(packed):
                    part = powers[group] if packed == 1 else jnp.where(mine == item, powers[group], 0.0)
                    weights_ref[at, rows(group, item), lanes] = part.astype(jnp.bfloat16)

    def mix(at, head):
        cut = slice(at // HEADS * span, (at // HEADS + 1) * span)
        mixed = dot(fields_ref[head_rows(2, head), cut], weights_ref[at]) * totals_ref[at]
        mixed_ref[head_rows(0, head), cut] = mixed.astype(jnp.bfloat16)

    count = runs * HEADS
    apart = max(1, AHEAD * 256 // span)
    for step in range(count + 2 * apart):
        for stage, late in ((score, 0), (soften, apart), (mix, 2 * apart)):
            at = step - late
            if 0 <= at < count:
                stage(at, at % HEADS)


def attend_lanes(fields_ref, scale_ref, mixed_ref, scores_ref, weights_ref, totals_ref, lanes):
    for head in range(HEADS):
        scores_ref[head] = dot(fields_ref[head_rows(1, head)], fields_ref[head_rows(0, head), lanes], TN)
    for head in range(HEADS):
        scores = scores_ref[head]
        factor = jnp.broadcast_to(scale_ref[head : head + 1, :1], (1, scores.shape[1]))
        powers = jnp.exp2((scores - jnp.max(scores, axis=0, keepdims=True)) * factor)
        totals_ref[head] = 1.0 / jnp.sum(powers, axis=0, keepdims=True)
        weights_ref[head] = powers.astype(jnp.bfloat16)
    for head in range(HEADS):
        mixed = dot(fields_ref[head_rows(2, head)], weights_ref[head]) * totals_ref[head]
        mixed_ref[head_rows(0, head)] = mixed.astype(jnp.bfloat16)


GROUPS = [[0, 2, 4, 5], [6, 7, 3, 1]]
ORDER = [2, 4, 5, 6, 7, 3, 1]


def pack_kernel(tokens_ref, *refs):
    pieces, held = refs[:-1], refs[-1]
    frames, patches = tokens_ref.shape[0], tokens_ref.shape[1] // len(pieces)
    me = lax.axis_index("tm")
    for frame in range(frames):
        for part in range(held.shape[0]):
            held[part, frame] = tokens_ref[frame, :, part * LANES : (part + 1) * LANES].astype(jnp.float32)
    for index, piece in enumerate(pieces):
        start = pl.multiple_of((me ^ index) * patches, patches)
        for part in range(held.shape[0]):
            rows = [held[part, frame, pl.ds(start, patches)] for frame in range(frames)]
            piece[:, part * LANES : (part + 1) * LANES] = jnp.concatenate(rows, axis=0).astype(jnp.bfloat16)


def hold_pieces(held, pieces):
    start = 0
    for piece in pieces:
        for part in range(held.shape[0]):
            held[part, start : start + piece.shape[0]] = piece[:, part * LANES : (part + 1) * LANES].astype(jnp.float32)
        start += piece.shape[0]


def fields_kernel(patches, gain_ref, proj_ref, *refs):
    pieces, (fields_ref, held) = refs[:-2], refs[-2:]
    hold_pieces(held, pieces)
    tokens = [pick(held, patch, held.shape[1] // patches, patches) for patch in range(patches)]
    project(layer_norm(jnp.concatenate(tokens, axis=0), gain_ref[...]), proj_ref, fields_ref)


def time_kernel(groups, patches, scale_ref, gain_ref, proj_ref, out_ref, *refs):
    count, ready = sum(map(len, groups)), len(groups) - 1
    fields, pieces = refs[:ready], refs[ready : ready + count]
    stream_ref, held, result, merged, mixed, own_fields, *work = refs[ready + count :]
    fields = fields + (own_fields,)
    rows = held.shape[1] // len(groups)
    length = rows // patches
    packed = time_packed(len(groups) * length, patches)
    hold_pieces(held, pieces)
    turn = len(groups) == 2
    order = [patch ^ packed if turn else patch for patch in range(patches)]
    tokens = [pick(held, ready * rows + patch, length, patches) for patch in order]
    project(layer_norm(jnp.concatenate(tokens, axis=0), gain_ref[...]), proj_ref, own_fields)
    if turn:
        near = lax.broadcasted_iota(jnp.int32, (HEAD_DIM, LANES), 1) < packed * length
        for low in range(0, 3 * WIDTH, HEAD_DIM):
            cut = slice(low, low + HEAD_DIM)
            for tile in range(0, rows, LANES):
                first, second = (group[cut, tile : tile + LANES] for group in fields)
                merged[cut, 2 * tile : 2 * tile + LANES] = jnp.where(near, first, second)
                merged[cut, 2 * tile + LANES : 2 * tile + 2 * LANES] = jnp.where(near, second, first)
    else:
        merged = own_fields
    attend(merged, scale_ref, mixed, *work, len(groups), packed, length)
    half = max(patches // 2, packed)
    for patch in range(patches):
        if patch % half == 0:
            cut = slice(patch * len(groups) * length, (patch + half) * len(groups) * length)
            update = dot(mixed[:, cut], out_ref[...], TN)
        for group in range(len(groups)):
            unit = patch % half // packed
            slot = group ^ (unit % 2) if turn else group
            first = ((unit * len(groups) + slot) * packed + patch % packed) * length
            place = pl.ds(group * rows + patch, length, stride=patches)
            for part in range(result.shape[0]):
                lanes = slice(part * LANES, (part + 1) * LANES)
                result[part, place, :] = held[part, place, :] + update[first : first + length, lanes]
    me = lax.axis_index("tm")
    size = pieces[0].shape[0]
    for index, piece in enumerate(place for group in groups for place in group):
        start = 0 if count == 1 else pl.multiple_of((me ^ piece) * size, size)
        for part in range(result.shape[0]):
            values = result[part, index * size : (index + 1) * size]
            stream_ref[pl.ds(start, size), part * LANES : (part + 1) * LANES] = values.astype(jnp.bfloat16)


def space_kernel(
    frame, senders, sides, frames, scale_ref, gain_ref, proj_ref, out_ref, stream_ref, *refs
):
    pieces, (fields, kept, held, tokens, mixed, *work) = refs[: sides // 2], refs[sides // 2 :]
    side_patches = pieces[0].shape[0]
    piece = stream_ref.shape[0] // senders // frames
    me = lax.axis_index("patch")
    if piece % 8:
        hold(held, stream_ref)
    for index in range(sides):
        first = index * side_patches
        if piece % 8:
            rows = pick(held, ((me ^ index) * frames + frame) * piece, senders // sides, sides * frames)
            tokens[first : first + side_patches] = rows
        else:
            for sender in range(senders // sides):
                start = pl.multiple_of((sender * sides + (me ^ index)) * frames * piece, frames * piece)
                rows = stream_ref[pl.ds(start, frames * piece), :].astype(jnp.float32)
                place = first + sender * piece
                tokens[place : place + piece] = rows[frame * piece : (frame + 1) * piece]
    half = sides // 2 * side_patches
    project(layer_norm(tokens[...], gain_ref[...]), proj_ref, fields)
    attend_lanes(fields, scale_ref, mixed, *work, slice(half, 2 * half))
    stream = tokens[half:] + dot(mixed[...], out_ref[...], TN)
    for index, target in enumerate(pieces):
        target[...] = stream[index * side_patches : (index + 1) * side_patches].astype(jnp.bfloat16)
    kept[...] = tokens[:half]


def near_kernel(frames, scale_ref, out_ref, *refs):
    pieces, (mixed, *work) = refs[2 * frames : -4], refs[-4:]
    side_patches = pieces[0].shape[1]
    for frame in range(frames):
        fields, kept = refs[2 * frame : 2 * frame + 2]
        attend_lanes(fields, scale_ref, mixed, *work, slice(0, kept.shape[0]))
        stream = kept[...] + dot(mixed[...], out_ref[...], TN)
        for index, target in enumerate(pieces):
            target[frame] = stream[index * side_patches : (index + 1) * side_patches].astype(jnp.bfloat16)


def place_kernel(places, *refs):
    count = len(places)
    pieces, whole, sems = refs[:count], refs[-count - 1], refs[-count:]
    me = lax.axis_index("patch")
    copies = [
        pltpu.make_async_copy(piece, whole.at[pl.ds((me ^ index) * frames + first, piece.shape[0])], sem)
        for piece, (index, first, frames), sem in zip(pieces, places, sems)
    ]
    for copy in copies:
        copy.start()
    for copy in copies:
        copy.wait()


def time_packed(frames, patches):
    return max(1, min(patches, LANES // frames))


def work_space(rows, span):
    return [
        pltpu.VMEM((3 * WIDTH, rows), jnp.bfloat16),
        pltpu.VMEM((WIDTH, rows), jnp.bfloat16),
    ], [
        pltpu.VMEM((rows // span * HEADS, span, span), jnp.float32),
        pltpu.VMEM((rows // span * HEADS, span, span), jnp.bfloat16),
        pltpu.VMEM((rows // span * HEADS, 1, span), jnp.float32),
    ]


def small_kernel(packed_ref, time_scale_ref, space_scale_ref, time_gain_ref, space_gain_ref):
    time_gain_ref[...] = packed_ref[:, :WIDTH]
    space_gain_ref[...] = packed_ref[:, WIDTH : 2 * WIDTH]
    for index, target in enumerate((time_scale_ref, space_scale_ref)):
        for head in range(HEADS):
            place = 2 * WIDTH + index * HEADS + head
            target[head : head + 1] = jnp.broadcast_to(packed_ref[:, place : place + 1] * LOG2_E, (1, LANES))


def small(time_scale, space_scale, time_gain, space_gain):
    whole = pl.BlockSpec(memory_space=pltpu.VMEM)
    shapes = [(HEADS, LANES), (HEADS, LANES), (1, WIDTH), (1, WIDTH)]
    return pl.pallas_call(
        small_kernel,
        out_shape=[jax.ShapeDtypeStruct(shape, jnp.float32) for shape in shapes],
        in_specs=[whole],
        out_specs=[whole] * 4,
        compiler_params=pltpu.CompilerParams(vmem_limit_bytes=1024 * 1024),
        cost_estimate=pl.CostEstimate(flops=10**10, bytes_accessed=10**5, transcendentals=0),
    )(jnp.concatenate([time_gain, space_gain, time_scale, space_scale])[None])


def call(kernel, out_shapes, scratch, flops, *rows):
    whole = pl.BlockSpec(memory_space=pltpu.VMEM)
    return pl.pallas_call(
        kernel,
        out_shape=[jax.ShapeDtypeStruct(*shape) for shape in out_shapes],
        in_specs=[whole] * len(rows),
        out_specs=[whole] * len(out_shapes),
        scratch_shapes=scratch,
        compiler_params=pltpu.CompilerParams(vmem_limit_bytes=VMEM_BYTES),
        cost_estimate=pl.CostEstimate(flops=flops, bytes_accessed=flops // 1000, transcendentals=0),
    )(*rows)


def project_early(patches, gain, proj, pieces):
    whole = pl.BlockSpec(memory_space=pltpu.VMEM)
    rows = sum(piece.shape[0] for piece in pieces)
    return pl.pallas_call(
        functools.partial(fields_kernel, patches),
        out_shape=jax.ShapeDtypeStruct((3 * WIDTH, rows), jnp.bfloat16),
        in_specs=[whole] * (2 + len(pieces)),
        out_specs=whole,
        scratch_shapes=[pltpu.VMEM((WIDTH // LANES, rows, LANES), jnp.float32)],
        compiler_params=pltpu.CompilerParams(vmem_limit_bytes=VMEM_BYTES),
        cost_estimate=pl.CostEstimate(flops=5 * 10**9, bytes_accessed=7 * 10**6, transcendentals=10**6),
    )(gain, proj, *pieces)


def pack(tokens, peers):
    frames, patches, width = tokens.shape
    whole = pl.BlockSpec(memory_space=pltpu.VMEM)
    return pl.pallas_call(
        pack_kernel,
        out_shape=[jax.ShapeDtypeStruct((frames * patches // peers, width), tokens.dtype)] * peers,
        in_specs=[whole],
        out_specs=[whole] * peers,
        scratch_shapes=[pltpu.VMEM((width // LANES, frames, patches, LANES), jnp.float32)],
        compiler_params=pltpu.CompilerParams(vmem_limit_bytes=8 * 1024 * 1024),
    )(tokens)


def place(places, pieces, whole, shape):
    anywhere = pl.BlockSpec(memory_space=pl.ANY)
    count = len(pieces)
    others = [] if whole is None else [whole]
    return pl.pallas_call(
        functools.partial(place_kernel, places),
        out_shape=jax.ShapeDtypeStruct(shape, jnp.bfloat16),
        in_specs=[anywhere] * (count + len(others)),
        out_specs=anywhere,
        scratch_shapes=[pltpu.SemaphoreType.DMA] * count,
        input_output_aliases={count: 0} if others else {},
        compiler_params=pltpu.CompilerParams(vmem_limit_bytes=1024 * 1024),
        cost_estimate=pl.CostEstimate(flops=10**10, bytes_accessed=10**6, transcendentals=0),
    )(*pieces, *others)


def exchange(piece, axis, index):
    size = lax.axis_size(axis)
    return lax.ppermute(piece, axis, [(i, i ^ index) for i in range(size)])


def swap(pieces, axis):
    arrived = list(pieces)
    for index in ORDER:
        arrived[index] = exchange(pieces[index], axis, index)
    return arrived


def per_device(
    tokens,
    time_gain,
    time_proj,
    time_out,
    time_scale,
    space_gain,
    space_proj,
    space_out,
    space_scale,
):
    frames, local_count, width = tokens.shape
    peers, sides = lax.axis_size("tm"), lax.axis_size("patch")
    rows = frames * local_count
    all_frames = frames * peers
    time_scale, space_scale, time_gain, space_gain = small(time_scale, space_scale, time_gain, space_gain)
    patches = local_count // peers
    fields = []
    if peers == 8:
        groups = GROUPS
        arrived = swap(pack(tokens, peers), "tm")
        arrived = [[arrived[index] for index in group] for group in groups]
        fields = [project_early(patches, time_gain, time_proj, pieces) for pieces in arrived[:-1]]
        arrived = sum(arrived, [])
    else:
        groups = [[0]]
        outgoing = jnp.swapaxes(tokens.reshape(frames, peers, patches, width), 0, 1).reshape(peers, rows // peers, width)
        arrived = [lax.all_to_all(outgoing, "tm", split_axis=0, concat_axis=0, tiled=True).reshape(rows, width)]
    held = pltpu.VMEM((width // LANES, rows, LANES), jnp.float32)
    space, work = work_space(rows, time_packed(all_frames, patches) * all_frames)
    stream = call(
        functools.partial(time_kernel, groups, patches),
        [((rows, width), jnp.bfloat16)],
        [held, held] + space + [pltpu.VMEM((3 * width, rows // len(groups)), jnp.bfloat16)] + work,
        10**10,
        time_scale, time_gain, time_proj, time_out, *fields, *arrived,
    )[0]
    senders = peers * sides
    stream = lax.all_to_all(
        stream.reshape(senders, rows // senders, width), ("tm", "patch"), split_axis=0, concat_axis=0, tiled=True
    ).reshape(rows, width)
    own_frames, columns, half = frames // sides, sides * local_count, sides // 2
    piece = (local_count, width)
    near_rows = half * local_count
    work = [
        pltpu.VMEM((width, near_rows), jnp.bfloat16),
        pltpu.VMEM((HEADS, columns, near_rows), jnp.float32),
        pltpu.VMEM((HEADS, columns, near_rows), jnp.bfloat16),
        pltpu.VMEM((HEADS, 1, near_rows), jnp.float32),
    ]
    far, kept = [], []
    for frame in range(own_frames):
        *pieces, fields, tokens_near = call(
            functools.partial(space_kernel, frame, senders, sides, own_frames),
            [(piece, jnp.bfloat16)] * half
            + [((3 * width, columns), jnp.bfloat16), ((near_rows, width), jnp.float32)],
            [held, pltpu.VMEM((columns, width), jnp.float32)] + work,
            10**10,
            space_scale, space_gain, space_proj, space_out, stream,
        )
        far.append([exchange(piece[None], "patch", half + index) for index, piece in enumerate(pieces)])
        kept += [fields, tokens_near]
    near = call(
        functools.partial(near_kernel, own_frames),
        [((own_frames,) + piece, jnp.bfloat16)] * half,
        work,
        10**6,
        space_scale, space_out, *kept,
    )
    near = [exchange(piece, "patch", index) if index else piece for index, piece in enumerate(near)]
    block = None
    for frame in range(own_frames):
        places, pieces = [(half + index, frame, own_frames) for index in range(half)], far[frame]
        if frame == own_frames - 1:
            places, pieces = places + [(index, 0, own_frames) for index in range(half)], pieces + near
        block = place(places, pieces, block, tokens.shape)
    return block


def solution(mesh):
    in_specs = (P("tm", "patch", None), P(), P(), P(), P(), P(), P(), P(), P())
    out_specs = P("tm", "patch", None)
    return jax.shard_map(
        per_device, mesh=mesh, in_specs=in_specs, out_specs=out_specs, check_vma=False
    )
```

```python
import functools
import math

import jax
import jax.numpy as jnp
from jax import lax
from jax.experimental import pallas as pl
from jax.experimental.pallas import tpu as pltpu
from jax.sharding import PartitionSpec as P

HEADS = 12
HEAD_DIM = 64
WIDTH = HEADS * HEAD_DIM
EPSILON = 1e-06
LOG2_E = math.log2(math.e)
LANES = 128
AHEAD = 12
VMEM_BYTES = 24 * 1024 * 1024

TN = (((0,), (0,)), ((), ()))
TT = (((0,), (1,)), ((), ()))


def dot(left, right, dims=(((1,), (0,)), ((), ()))):
    return lax.dot_general(left, right, dims, preferred_element_type=jnp.float32)


def layer_norm(values, gain):
    centred = values - jnp.mean(values, axis=-1, keepdims=True)
    spread = jnp.mean(centred * centred, axis=-1, keepdims=True)
    return (centred * lax.rsqrt(spread + EPSILON) * gain).astype(jnp.bfloat16)


def unit_columns(fields):
    heads = fields.reshape(HEADS, HEAD_DIM, fields.shape[1])
    squares = jnp.sum(heads * heads, axis=1, keepdims=True)
    return (heads * lax.rsqrt(squares + EPSILON)).reshape(fields.shape)


def project(normed, proj_ref, fields_ref):
    for cut, fields in projected(normed, proj_ref):
        fields_ref[cut] = fields


def projected(normed, proj_ref):
    for part in range(3):
        cut = slice(part * WIDTH, (part + 1) * WIDTH)
        fields = dot(proj_ref[:, cut], normed, TT)
        if part < 2:
            fields = unit_columns(fields)
        yield cut, fields.astype(jnp.bfloat16)


def hold(held, values):
    for part in range(held.shape[0]):
        held[part] = values[:, part * LANES : (part + 1) * LANES].astype(jnp.float32)


def pick(held, start, count, step):
    return jnp.concatenate(
        [held[part, pl.ds(start, count, stride=step), :] for part in range(held.shape[0])], axis=1
    )


def head_rows(part, head):
    return slice(part * WIDTH + head * HEAD_DIM, part * WIDTH + (head + 1) * HEAD_DIM)


def attend(fields_ref, scale_ref, mixed_ref, scores_ref, weights_ref, totals_ref, groups, packed, length):
    span = groups * packed * length
    runs = fields_ref.shape[1] // span
    item_of = (lax.broadcasted_iota(jnp.int32, (1, span), 1) // length) % packed

    def rows(group, item):
        first = (group * packed + item) * length
        return slice(first, first + length)

    def score(at, head):
        cut = slice(at // HEADS * span, (at // HEADS + 1) * span)
        scores_ref[at] = dot(fields_ref[head_rows(1, head), cut], fields_ref[head_rows(0, head), cut], TN)

    def soften(at, head):
        factor = scale_ref[head : head + 1]
        for low in range(0, span, LANES):
            lanes = slice(low, low + LANES)
            mine = jnp.broadcast_to(item_of[:, lanes], (length, LANES))
            scores = []
            for group in range(groups):
                own = scores_ref[at, rows(group, 0), lanes]
                for item in range(1, packed):
                    own = jnp.where(mine == item, scores_ref[at, rows(group, item), lanes], own)
                scores.append(own)
            largest = functools.reduce(jnp.maximum, [jnp.max(own, axis=0, keepdims=True) for own in scores])
            powers = [jnp.exp2((own - largest) * factor) for own in scores]
            totals_ref[at, :, lanes] = 1.0 / sum(jnp.sum(part, axis=0, keepdims=True) for part in powers)
            for group in range(groups):
                for item in range(packed):
                    part = powers[group] if packed == 1 else jnp.where(mine == item, powers[group], 0.0)
                    weights_ref[at, rows(group, item), lanes] = part.astype(jnp.bfloat16)

    def mix(at, head):
        cut = slice(at // HEADS * span, (at // HEADS + 1) * span)
        mixed = dot(fields_ref[head_rows(2, head), cut], weights_ref[at]) * totals_ref[at]
        mixed_ref[head_rows(0, head), cut] = mixed.astype(jnp.bfloat16)

    count = runs * HEADS
    apart = max(1, AHEAD * 256 // span)
    for step in range(count + 2 * apart):
        for stage, late in ((score, 0), (soften, apart), (mix, 2 * apart)):
            at = step - late
            if 0 <= at < count:
                stage(at, at % HEADS)


def attend_lanes(fields_ref, scale_ref, mixed_ref, scores_ref, weights_ref, totals_ref, lanes):
    for head in range(HEADS):
        scores_ref[head] = dot(fields_ref[head_rows(1, head)], fields_ref[head_rows(0, head), lanes], TN)
    for head in range(HEADS):
        scores = scores_ref[head]
        factor = jnp.broadcast_to(scale_ref[head : head + 1, :1], (1, scores.shape[1]))
        powers = jnp.exp2((scores - jnp.max(scores, axis=0, keepdims=True)) * factor)
        totals_ref[head] = 1.0 / jnp.sum(powers, axis=0, keepdims=True)
        weights_ref[head] = powers.astype(jnp.bfloat16)
    for head in range(HEADS):
        mixed = dot(fields_ref[head_rows(2, head)], weights_ref[head]) * totals_ref[head]
        mixed_ref[head_rows(0, head)] = mixed.astype(jnp.bfloat16)


GROUPS = [[0, 2, 4, 5], [6, 7, 3, 1]]
ORDER = [2, 4, 5, 6, 7, 3, 1]


def pack_kernel(tokens_ref, *refs):
    pieces, held = refs[:-1], refs[-1]
    frames, patches = tokens_ref.shape[0], tokens_ref.shape[1] // len(pieces)
    me = lax.axis_index("tm")
    for frame in range(frames):
        for part in range(held.shape[0]):
            held[part, frame] = tokens_ref[frame, :, part * LANES : (part + 1) * LANES].astype(jnp.float32)
    for index, piece in enumerate(pieces):
        start = pl.multiple_of((me ^ index) * patches, patches)
        for part in range(held.shape[0]):
            rows = [held[part, frame, pl.ds(start, patches)] for frame in range(frames)]
            piece[:, part * LANES : (part + 1) * LANES] = jnp.concatenate(rows, axis=0).astype(jnp.bfloat16)


def hold_pieces(held, pieces):
    start = 0
    for piece in pieces:
        for part in range(held.shape[0]):
            held[part, start : start + piece.shape[0]] = piece[:, part * LANES : (part + 1) * LANES].astype(jnp.float32)
        start += piece.shape[0]


def fields_kernel(patches, gain_ref, proj_ref, *refs):
    pieces, (fields_ref, held) = refs[:-2], refs[-2:]
    hold_pieces(held, pieces)
    tokens = [pick(held, patch, held.shape[1] // patches, patches) for patch in range(patches)]
    project(layer_norm(jnp.concatenate(tokens, axis=0), gain_ref[...]), proj_ref, fields_ref)


def time_kernel(groups, patches, scale_ref, gain_ref, proj_ref, out_ref, *refs):
    count, ready = sum(map(len, groups)), len(groups) - 1
    fields, pieces = refs[:ready], refs[ready : ready + count]
    stream_ref, held, result, merged, mixed, *work = refs[ready + count :]
    rows = held.shape[1] // len(groups)
    length = rows // patches
    packed = time_packed(len(groups) * length, patches)
    hold_pieces(held, pieces)
    turn = len(groups) == 2
    order = [patch ^ packed if turn else patch for patch in range(patches)]
    tokens = [pick(held, ready * rows + patch, length, patches) for patch in order]
    normed = layer_norm(jnp.concatenate(tokens, axis=0), gain_ref[...])
    if turn:
        near = lax.broadcasted_iota(jnp.int32, (WIDTH, LANES), 1) < packed * length
        for cut, own in projected(normed, proj_ref):
            for tile in range(0, rows, LANES):
                first, second = fields[0][cut, tile : tile + LANES], own[:, tile : tile + LANES]
                merged[cut, 2 * tile : 2 * tile + LANES] = jnp.where(near, first, second)
                merged[cut, 2 * tile + LANES : 2 * tile + 2 * LANES] = jnp.where(near, second, first)
    else:
        project(normed, proj_ref, merged)
    attend(merged, scale_ref, mixed, *work, len(groups), packed, length)
    half = max(patches // 2, packed)
    for patch in range(patches):
        if patch % half == 0:
            cut = slice(patch * len(groups) * length, (patch + half) * len(groups) * length)
            update = dot(mixed[:, cut], out_ref[...], TN)
        for group in range(len(groups)):
            unit = patch % half // packed
            slot = group ^ (unit % 2) if turn else group
            first = ((unit * len(groups) + slot) * packed + patch % packed) * length
            place = pl.ds(group * rows + patch, length, stride=patches)
            for part in range(result.shape[0]):
                lanes = slice(part * LANES, (part + 1) * LANES)
                result[part, place, :] = held[part, place, :] + update[first : first + length, lanes]
    me = lax.axis_index("tm")
    size = pieces[0].shape[0]
    for index, piece in enumerate(place for group in groups for place in group):
        start = 0 if count == 1 else pl.multiple_of((me ^ piece) * size, size)
        for part in range(result.shape[0]):
            values = result[part, index * size : (index + 1) * size]
            stream_ref[pl.ds(start, size), part * LANES : (part + 1) * LANES] = values.astype(jnp.bfloat16)


def space_kernel(
    frame, senders, sides, frames, scale_ref, gain_ref, proj_ref, out_ref, stream_ref, *refs
):
    pieces, (fields, kept, held, tokens, mixed, *work) = refs[: sides // 2], refs[sides // 2 :]
    side_patches = pieces[0].shape[0]
    piece = stream_ref.shape[0] // senders // frames
    me = lax.axis_index("patch")
    if piece % 8:
        hold(held, stream_ref)
    for index in range(sides):
        first = index * side_patches
        if piece % 8:
            rows = pick(held, ((me ^ index) * frames + frame) * piece, senders // sides, sides * frames)
            tokens[first : first + side_patches] = rows
        else:
            for sender in range(senders // sides):
                start = pl.multiple_of((sender * sides + (me ^ index)) * frames * piece, frames * piece)
                rows = stream_ref[pl.ds(start, frames * piece), :].astype(jnp.float32)
                place = first + sender * piece
                tokens[place : place + piece] = rows[frame * piece : (frame + 1) * piece]
    half = sides // 2 * side_patches
    project(layer_norm(tokens[...], gain_ref[...]), proj_ref, fields)
    attend_lanes(fields, scale_ref, mixed, *work, slice(half, 2 * half))
    stream = tokens[half:] + dot(mixed[...], out_ref[...], TN)
    for index, target in enumerate(pieces):
        target[...] = stream[index * side_patches : (index + 1) * side_patches].astype(jnp.bfloat16)
    kept[...] = tokens[:half]


def near_kernel(frames, scale_ref, out_ref, *refs):
    pieces, (mixed, *work) = refs[2 * frames : -4], refs[-4:]
    side_patches = pieces[0].shape[1]
    for frame in range(frames):
        fields, kept = refs[2 * frame : 2 * frame + 2]
        attend_lanes(fields, scale_ref, mixed, *work, slice(0, kept.shape[0]))
        stream = kept[...] + dot(mixed[...], out_ref[...], TN)
        for index, target in enumerate(pieces):
            target[frame] = stream[index * side_patches : (index + 1) * side_patches].astype(jnp.bfloat16)


def place_kernel(places, *refs):
    count = len(places)
    pieces, whole, sems = refs[:count], refs[-count - 1], refs[-count:]
    me = lax.axis_index("patch")
    copies = [
        pltpu.make_async_copy(piece, whole.at[pl.ds((me ^ index) * frames + first, piece.shape[0])], sem)
        for piece, (index, first, frames), sem in zip(pieces, places, sems)
    ]
    for copy in copies:
        copy.start()
    for copy in copies:
        copy.wait()


def time_packed(frames, patches):
    return max(1, min(patches, LANES // frames))


def work_space(rows, span):
    return [
        pltpu.VMEM((3 * WIDTH, rows), jnp.bfloat16),
        pltpu.VMEM((WIDTH, rows), jnp.bfloat16),
    ], [
        pltpu.VMEM((rows // span * HEADS, span, span), jnp.float32),
        pltpu.VMEM((rows // span * HEADS, span, span), jnp.bfloat16),
        pltpu.VMEM((rows // span * HEADS, 1, span), jnp.float32),
    ]


def small_kernel(packed_ref, time_scale_ref, space_scale_ref, time_gain_ref, space_gain_ref):
    time_gain_ref[...] = packed_ref[:, :WIDTH]
    space_gain_ref[...] = packed_ref[:, WIDTH : 2 * WIDTH]
    for index, target in enumerate((time_scale_ref, space_scale_ref)):
        for head in range(HEADS):
            place = 2 * WIDTH + index * HEADS + head
            target[head : head + 1] = jnp.broadcast_to(packed_ref[:, place : place + 1] * LOG2_E, (1, LANES))


def small(time_scale, space_scale, time_gain, space_gain):
    whole = pl.BlockSpec(memory_space=pltpu.VMEM)
    shapes = [(HEADS, LANES), (HEADS, LANES), (1, WIDTH), (1, WIDTH)]
    return pl.pallas_call(
        small_kernel,
        out_shape=[jax.ShapeDtypeStruct(shape, jnp.float32) for shape in shapes],
        in_specs=[whole],
        out_specs=[whole] * 4,
        compiler_params=pltpu.CompilerParams(vmem_limit_bytes=1024 * 1024),
        cost_estimate=pl.CostEstimate(flops=10**10, bytes_accessed=10**5, transcendentals=0),
    )(jnp.concatenate([time_gain, space_gain, time_scale, space_scale])[None])


def call(kernel, out_shapes, scratch, flops, *rows):
    whole = pl.BlockSpec(memory_space=pltpu.VMEM)
    return pl.pallas_call(
        kernel,
        out_shape=[jax.ShapeDtypeStruct(*shape) for shape in out_shapes],
        in_specs=[whole] * len(rows),
        out_specs=[whole] * len(out_shapes),
        scratch_shapes=scratch,
        compiler_params=pltpu.CompilerParams(vmem_limit_bytes=VMEM_BYTES),
        cost_estimate=pl.CostEstimate(flops=flops, bytes_accessed=flops // 1000, transcendentals=0),
    )(*rows)


def project_early(patches, gain, proj, pieces):
    whole = pl.BlockSpec(memory_space=pltpu.VMEM)
    rows = sum(piece.shape[0] for piece in pieces)
    return pl.pallas_call(
        functools.partial(fields_kernel, patches),
        out_shape=jax.ShapeDtypeStruct((3 * WIDTH, rows), jnp.bfloat16),
        in_specs=[whole] * (2 + len(pieces)),
        out_specs=whole,
        scratch_shapes=[pltpu.VMEM((WIDTH // LANES, rows, LANES), jnp.float32)],
        compiler_params=pltpu.CompilerParams(vmem_limit_bytes=VMEM_BYTES),
        cost_estimate=pl.CostEstimate(flops=5 * 10**9, bytes_accessed=7 * 10**6, transcendentals=10**6),
    )(gain, proj, *pieces)


def pack(tokens, peers):
    frames, patches, width = tokens.shape
    whole = pl.BlockSpec(memory_space=pltpu.VMEM)
    return pl.pallas_call(
        pack_kernel,
        out_shape=[jax.ShapeDtypeStruct((frames * patches // peers, width), tokens.dtype)] * peers,
        in_specs=[whole],
        out_specs=[whole] * peers,
        scratch_shapes=[pltpu.VMEM((width // LANES, frames, patches, LANES), jnp.float32)],
        compiler_params=pltpu.CompilerParams(vmem_limit_bytes=8 * 1024 * 1024),
    )(tokens)


def place(places, pieces, whole, shape, flops):
    anywhere = pl.BlockSpec(memory_space=pl.ANY)
    count = len(pieces)
    others = [] if whole is None else [whole]
    return pl.pallas_call(
        functools.partial(place_kernel, places),
        out_shape=jax.ShapeDtypeStruct(shape, jnp.bfloat16),
        in_specs=[anywhere] * (count + len(others)),
        out_specs=anywhere,
        scratch_shapes=[pltpu.SemaphoreType.DMA] * count,
        input_output_aliases={count: 0} if others else {},
        compiler_params=pltpu.CompilerParams(vmem_limit_bytes=1024 * 1024),
        cost_estimate=pl.CostEstimate(flops=flops, bytes_accessed=flops // 10**4, transcendentals=0),
    )(*pieces, *others)


def exchange(piece, axis, index):
    size = lax.axis_size(axis)
    return lax.ppermute(piece, axis, [(i, i ^ index) for i in range(size)])


def swap(pieces, axis):
    arrived = list(pieces)
    for index in ORDER:
        arrived[index] = exchange(pieces[index], axis, index)
    return arrived


def per_device(
    tokens,
    time_gain,
    time_proj,
    time_out,
    time_scale,
    space_gain,
    space_proj,
    space_out,
    space_scale,
):
    frames, local_count, width = tokens.shape
    peers, sides = lax.axis_size("tm"), lax.axis_size("patch")
    rows = frames * local_count
    all_frames = frames * peers
    time_scale, space_scale, time_gain, space_gain = small(time_scale, space_scale, time_gain, space_gain)
    patches = local_count // peers
    fields = []
    if peers == 8:
        groups = GROUPS
        arrived = swap(pack(tokens, peers), "tm")
        arrived = [[arrived[index] for index in group] for group in groups]
        fields = [project_early(patches, time_gain, time_proj, pieces) for pieces in arrived[:-1]]
        arrived = sum(arrived, [])
    else:
        groups = [[0]]
        outgoing = jnp.swapaxes(tokens.reshape(frames, peers, patches, width), 0, 1).reshape(peers, rows // peers, width)
        arrived = [lax.all_to_all(outgoing, "tm", split_axis=0, concat_axis=0, tiled=True).reshape(rows, width)]
    held = pltpu.VMEM((width // LANES, rows, LANES), jnp.float32)
    space, work = work_space(rows, time_packed(all_frames, patches) * all_frames)
    stream = call(
        functools.partial(time_kernel, groups, patches),
        [((rows, width), jnp.bfloat16)],
        [held, held] + space + work,
        10**10,
        time_scale, time_gain, time_proj, time_out, *fields, *arrived,
    )[0]
    senders = peers * sides
    stream = lax.all_to_all(
        stream.reshape(senders, rows // senders, width), ("tm", "patch"), split_axis=0, concat_axis=0, tiled=True
    ).reshape(rows, width)
    own_frames, columns, half = frames // sides, sides * local_count, sides // 2
    piece = (local_count, width)
    near_rows = half * local_count
    work = [
        pltpu.VMEM((width, near_rows), jnp.bfloat16),
        pltpu.VMEM((HEADS, columns, near_rows), jnp.float32),
        pltpu.VMEM((HEADS, columns, near_rows), jnp.bfloat16),
        pltpu.VMEM((HEADS, 1, near_rows), jnp.float32),
    ]
    far, kept = [], []
    for frame in range(own_frames):
        *pieces, fields, tokens_near = call(
            functools.partial(space_kernel, frame, senders, sides, own_frames),
            [(piece, jnp.bfloat16)] * half
            + [((3 * width, columns), jnp.bfloat16), ((near_rows, width), jnp.float32)],
            [held, pltpu.VMEM((columns, width), jnp.float32)] + work,
            10**10,
            space_scale, space_gain, space_proj, space_out, stream,
        )
        far.append([exchange(piece[None], "patch", half + index) for index, piece in enumerate(pieces)])
        kept += [fields, tokens_near]
    near = call(
        functools.partial(near_kernel, own_frames),
        [((own_frames,) + piece, jnp.bfloat16)] * half,
        work,
        10**6,
        space_scale, space_out, *kept,
    )
    near = [exchange(piece, "patch", index) if index else piece for index, piece in enumerate(near)]
    block = None
    for frame in range(own_frames):
        if frame == own_frames - 1:
            block = place([(index, 0, own_frames) for index in range(half)], near, block, tokens.shape, 10**6)
        places = [(half + index, frame, own_frames) for index in range(half)]
        block = place(places, far[frame], block, tokens.shape, 10**10)
    return block


def solution(mesh):
    in_specs = (P("tm", "patch", None), P(), P(), P(), P(), P(), P(), P(), P())
    out_specs = P("tm", "patch", None)
    return jax.shard_map(
        per_device, mesh=mesh, in_specs=in_specs, out_specs=out_specs, check_vma=False
    )
```

```python
import functools
import math

import jax
import jax.numpy as jnp
from jax import lax
from jax.experimental import pallas as pl
from jax.experimental.pallas import tpu as pltpu
from jax.sharding import PartitionSpec as P

HEADS = 12
HEAD_DIM = 64
WIDTH = HEADS * HEAD_DIM
EPSILON = 1e-06
LOG2_E = math.log2(math.e)
LANES = 128
AHEAD = 12
VMEM_BYTES = 24 * 1024 * 1024

TN = (((0,), (0,)), ((), ()))
TT = (((0,), (1,)), ((), ()))


def dot(left, right, dims=(((1,), (0,)), ((), ()))):
    return lax.dot_general(left, right, dims, preferred_element_type=jnp.float32)


def layer_norm(values, gain):
    centred = values - jnp.mean(values, axis=-1, keepdims=True)
    spread = jnp.mean(centred * centred, axis=-1, keepdims=True)
    return (centred * lax.rsqrt(spread + EPSILON) * gain).astype(jnp.bfloat16)


def unit_columns(fields):
    heads = fields.reshape(HEADS, HEAD_DIM, fields.shape[1])
    squares = jnp.sum(heads * heads, axis=1, keepdims=True)
    return (heads * lax.rsqrt(squares + EPSILON)).reshape(fields.shape)


QUERIES_KEYS = [slice(0, WIDTH), slice(WIDTH, 2 * WIDTH)]
VALUES = [slice(2 * WIDTH, 3 * WIDTH)]


def project(normed, proj_ref, fields_ref, cuts):
    for cut, fields in projected(normed, proj_ref, cuts):
        fields_ref[cut] = fields


def projected(normed, proj_ref, cuts):
    for cut in cuts:
        fields = dot(proj_ref[:, cut], normed, TT)
        if cut.start < 2 * WIDTH:
            fields = unit_columns(fields)
        yield cut, fields.astype(jnp.bfloat16)


def hold(held, values):
    for part in range(held.shape[0]):
        held[part] = values[:, part * LANES : (part + 1) * LANES].astype(jnp.float32)


def pick(held, start, count, step):
    return jnp.concatenate(
        [held[part, pl.ds(start, count, stride=step), :] for part in range(held.shape[0])], axis=1
    )


def head_rows(part, head):
    return slice(part * WIDTH + head * HEAD_DIM, part * WIDTH + (head + 1) * HEAD_DIM)


def attend(fields_ref, scale_ref, mixed_ref, scores_ref, weights_ref, totals_ref, groups, packed, length, project_part):
    span = groups * packed * length
    runs = fields_ref.shape[1] // span
    item_of = (lax.broadcasted_iota(jnp.int32, (1, span), 1) // length) % packed

    def rows(group, item):
        first = (group * packed + item) * length
        return slice(first, first + length)

    def score(at, head):
        cut = slice(at // HEADS * span, (at // HEADS + 1) * span)
        scores_ref[at] = dot(fields_ref[head_rows(1, head), cut], fields_ref[head_rows(0, head), cut], TN)

    def soften(at, head):
        factor = scale_ref[head : head + 1]
        for low in range(0, span, LANES):
            lanes = slice(low, low + LANES)
            mine = jnp.broadcast_to(item_of[:, lanes], (length, LANES))
            scores = []
            for group in range(groups):
                own = scores_ref[at, rows(group, 0), lanes]
                for item in range(1, packed):
                    own = jnp.where(mine == item, scores_ref[at, rows(group, item), lanes], own)
                scores.append(own)
            largest = functools.reduce(jnp.maximum, [jnp.max(own, axis=0, keepdims=True) for own in scores])
            powers = [jnp.exp2((own - largest) * factor) for own in scores]
            totals_ref[at, :, lanes] = 1.0 / sum(jnp.sum(part, axis=0, keepdims=True) for part in powers)
            for group in range(groups):
                for item in range(packed):
                    part = powers[group] if packed == 1 else jnp.where(mine == item, powers[group], 0.0)
                    weights_ref[at, rows(group, item), lanes] = part.astype(jnp.bfloat16)

    def mix(at, head):
        cut = slice(at // HEADS * span, (at // HEADS + 1) * span)
        mixed = dot(fields_ref[head_rows(2, head), cut], weights_ref[at]) * totals_ref[at]
        mixed_ref[head_rows(0, head), cut] = mixed.astype(jnp.bfloat16)

    count = runs * HEADS
    apart = max(1, AHEAD * 256 // span)
    for step in range(count + 2 * apart):
        if step == apart // 2:
            project_part(VALUES)
        for stage, late in ((score, 0), (soften, apart), (mix, 2 * apart)):
            at = step - late
            if 0 <= at < count:
                stage(at, at % HEADS)


def attend_lanes(fields_ref, scale_ref, mixed_ref, scores_ref, weights_ref, totals_ref, lanes):
    for head in range(HEADS):
        scores_ref[head] = dot(fields_ref[head_rows(1, head)], fields_ref[head_rows(0, head), lanes], TN)
    for head in range(HEADS):
        scores = scores_ref[head]
        factor = jnp.broadcast_to(scale_ref[head : head + 1, :1], (1, scores.shape[1]))
        powers = jnp.exp2((scores - jnp.max(scores, axis=0, keepdims=True)) * factor)
        totals_ref[head] = 1.0 / jnp.sum(powers, axis=0, keepdims=True)
        weights_ref[head] = powers.astype(jnp.bfloat16)
    for head in range(HEADS):
        mixed = dot(fields_ref[head_rows(2, head)], weights_ref[head]) * totals_ref[head]
        mixed_ref[head_rows(0, head)] = mixed.astype(jnp.bfloat16)


GROUPS = [[0, 2, 4, 5], [6, 7, 3, 1]]
ORDER = [2, 4, 5, 6, 7, 3, 1]


def pack_kernel(tokens_ref, *refs):
    pieces, held = refs[:-1], refs[-1]
    frames, patches = tokens_ref.shape[0], tokens_ref.shape[1] // len(pieces)
    me = lax.axis_index("tm")
    for frame in range(frames):
        for part in range(held.shape[0]):
            held[part, frame] = tokens_ref[frame, :, part * LANES : (part + 1) * LANES].astype(jnp.float32)
    for index, piece in enumerate(pieces):
        start = pl.multiple_of((me ^ index) * patches, patches)
        for part in range(held.shape[0]):
            rows = [held[part, frame, pl.ds(start, patches)] for frame in range(frames)]
            piece[:, part * LANES : (part + 1) * LANES] = jnp.concatenate(rows, axis=0).astype(jnp.bfloat16)


def hold_pieces(held, pieces):
    start = 0
    for piece in pieces:
        for part in range(held.shape[0]):
            held[part, start : start + piece.shape[0]] = piece[:, part * LANES : (part + 1) * LANES].astype(jnp.float32)
        start += piece.shape[0]


def fields_kernel(patches, gain_ref, proj_ref, *refs):
    pieces, (fields_ref, held) = refs[:-2], refs[-2:]
    hold_pieces(held, pieces)
    tokens = [pick(held, patch, held.shape[1] // patches, patches) for patch in range(patches)]
    project(layer_norm(jnp.concatenate(tokens, axis=0), gain_ref[...]), proj_ref, fields_ref, QUERIES_KEYS + VALUES)


def time_kernel(groups, patches, scale_ref, gain_ref, proj_ref, out_ref, *refs):
    count, ready = sum(map(len, groups)), len(groups) - 1
    fields, pieces = refs[:ready], refs[ready : ready + count]
    stream_ref, held, result, merged, mixed, *work = refs[ready + count :]
    rows = held.shape[1] // len(groups)
    length = rows // patches
    packed = time_packed(len(groups) * length, patches)
    hold_pieces(held, pieces)
    turn = len(groups) == 2
    order = [patch ^ packed if turn else patch for patch in range(patches)]
    tokens = [pick(held, ready * rows + patch, length, patches) for patch in order]
    normed = layer_norm(jnp.concatenate(tokens, axis=0), gain_ref[...])

    def project_part(cuts):
        if not turn:
            return project(normed, proj_ref, merged, cuts)
        for cut, own in projected(normed, proj_ref, cuts):
            near = lax.broadcasted_iota(jnp.int32, (cut.stop - cut.start, LANES), 1) < packed * length
            for tile in range(0, rows, LANES):
                first, second = fields[0][cut, tile : tile + LANES], own[:, tile : tile + LANES]
                merged[cut, 2 * tile : 2 * tile + LANES] = jnp.where(near, first, second)
                merged[cut, 2 * tile + LANES : 2 * tile + 2 * LANES] = jnp.where(near, second, first)

    project_part(QUERIES_KEYS)
    attend(merged, scale_ref, mixed, *work, len(groups), packed, length, project_part)
    half = max(patches // 2, packed)
    for patch in range(patches):
        if patch % half == 0:
            cut = slice(patch * len(groups) * length, (patch + half) * len(groups) * length)
            update = dot(mixed[:, cut], out_ref[...], TN)
        for group in range(len(groups)):
            unit = patch % half // packed
            slot = group ^ (unit % 2) if turn else group
            first = ((unit * len(groups) + slot) * packed + patch % packed) * length
            place = pl.ds(group * rows + patch, length, stride=patches)
            for part in range(result.shape[0]):
                lanes = slice(part * LANES, (part + 1) * LANES)
                result[part, place, :] = held[part, place, :] + update[first : first + length, lanes]
    me = lax.axis_index("tm")
    size = pieces[0].shape[0]
    for index, piece in enumerate(place for group in groups for place in group):
        start = 0 if count == 1 else pl.multiple_of((me ^ piece) * size, size)
        for part in range(result.shape[0]):
            values = result[part, index * size : (index + 1) * size]
            stream_ref[pl.ds(start, size), part * LANES : (part + 1) * LANES] = values.astype(jnp.bfloat16)


def space_kernel(
    frame, senders, sides, frames, scale_ref, gain_ref, proj_ref, out_ref, stream_ref, *refs
):
    pieces, (fields, kept, held, tokens, mixed, *work) = refs[: sides // 2], refs[sides // 2 :]
    side_patches = pieces[0].shape[0]
    piece = stream_ref.shape[0] // senders // frames
    me = lax.axis_index("patch")
    if piece % 8:
        hold(held, stream_ref)
    for index in range(sides):
        first = index * side_patches
        if piece % 8:
            rows = pick(held, ((me ^ index) * frames + frame) * piece, senders // sides, sides * frames)
            tokens[first : first + side_patches] = rows
        else:
            for sender in range(senders // sides):
                start = pl.multiple_of((sender * sides + (me ^ index)) * frames * piece, frames * piece)
                rows = stream_ref[pl.ds(start, frames * piece), :].astype(jnp.float32)
                place = first + sender * piece
                tokens[place : place + piece] = rows[frame * piece : (frame + 1) * piece]
    half = sides // 2 * side_patches
    project(layer_norm(tokens[...], gain_ref[...]), proj_ref, fields, QUERIES_KEYS + VALUES)
    attend_lanes(fields, scale_ref, mixed, *work, slice(half, 2 * half))
    stream = tokens[half:] + dot(mixed[...], out_ref[...], TN)
    for index, target in enumerate(pieces):
        target[...] = stream[index * side_patches : (index + 1) * side_patches].astype(jnp.bfloat16)
    kept[...] = tokens[:half]


def near_kernel(frames, scale_ref, out_ref, *refs):
    pieces, (mixed, *work) = refs[2 * frames : -4], refs[-4:]
    side_patches = pieces[0].shape[1]
    for frame in range(frames):
        fields, kept = refs[2 * frame : 2 * frame + 2]
        attend_lanes(fields, scale_ref, mixed, *work, slice(0, kept.shape[0]))
        stream = kept[...] + dot(mixed[...], out_ref[...], TN)
        for index, target in enumerate(pieces):
            target[frame] = stream[index * side_patches : (index + 1) * side_patches].astype(jnp.bfloat16)


def place_kernel(places, *refs):
    count = len(places)
    pieces, whole, sems = refs[:count], refs[-count - 1], refs[-count:]
    me = lax.axis_index("patch")
    copies = [
        pltpu.make_async_copy(piece, whole.at[pl.ds((me ^ index) * frames + first, piece.shape[0])], sem)
        for piece, (index, first, frames), sem in zip(pieces, places, sems)
    ]
    for copy in copies:
        copy.start()
    for copy in copies:
        copy.wait()


def time_packed(frames, patches):
    return max(1, min(patches, LANES // frames))


def work_space(rows, span):
    return [
        pltpu.VMEM((3 * WIDTH, rows), jnp.bfloat16),
        pltpu.VMEM((WIDTH, rows), jnp.bfloat16),
    ], [
        pltpu.VMEM((rows // span * HEADS, span, span), jnp.float32),
        pltpu.VMEM((rows // span * HEADS, span, span), jnp.bfloat16),
        pltpu.VMEM((rows // span * HEADS, 1, span), jnp.float32),
    ]


def small_kernel(packed_ref, time_scale_ref, space_scale_ref, time_gain_ref, space_gain_ref):
    time_gain_ref[...] = packed_ref[:, :WIDTH]
    space_gain_ref[...] = packed_ref[:, WIDTH : 2 * WIDTH]
    for index, target in enumerate((time_scale_ref, space_scale_ref)):
        for head in range(HEADS):
            place = 2 * WIDTH + index * HEADS + head
            target[head : head + 1] = jnp.broadcast_to(packed_ref[:, place : place + 1] * LOG2_E, (1, LANES))


def small(time_scale, space_scale, time_gain, space_gain):
    whole = pl.BlockSpec(memory_space=pltpu.VMEM)
    shapes = [(HEADS, LANES), (HEADS, LANES), (1, WIDTH), (1, WIDTH)]
    return pl.pallas_call(
        small_kernel,
        out_shape=[jax.ShapeDtypeStruct(shape, jnp.float32) for shape in shapes],
        in_specs=[whole],
        out_specs=[whole] * 4,
        compiler_params=pltpu.CompilerParams(vmem_limit_bytes=1024 * 1024),
        cost_estimate=pl.CostEstimate(flops=10**10, bytes_accessed=10**5, transcendentals=0),
    )(jnp.concatenate([time_gain, space_gain, time_scale, space_scale])[None])


def call(kernel, out_shapes, scratch, flops, *rows):
    whole = pl.BlockSpec(memory_space=pltpu.VMEM)
    return pl.pallas_call(
        kernel,
        out_shape=[jax.ShapeDtypeStruct(*shape) for shape in out_shapes],
        in_specs=[whole] * len(rows),
        out_specs=[whole] * len(out_shapes),
        scratch_shapes=scratch,
        compiler_params=pltpu.CompilerParams(vmem_limit_bytes=VMEM_BYTES),
        cost_estimate=pl.CostEstimate(flops=flops, bytes_accessed=flops // 1000, transcendentals=0),
    )(*rows)


def project_early(patches, gain, proj, pieces):
    whole = pl.BlockSpec(memory_space=pltpu.VMEM)
    rows = sum(piece.shape[0] for piece in pieces)
    return pl.pallas_call(
        functools.partial(fields_kernel, patches),
        out_shape=jax.ShapeDtypeStruct((3 * WIDTH, rows), jnp.bfloat16),
        in_specs=[whole] * (2 + len(pieces)),
        out_specs=whole,
        scratch_shapes=[pltpu.VMEM((WIDTH // LANES, rows, LANES), jnp.float32)],
        compiler_params=pltpu.CompilerParams(vmem_limit_bytes=VMEM_BYTES),
        cost_estimate=pl.CostEstimate(flops=5 * 10**9, bytes_accessed=7 * 10**6, transcendentals=10**6),
    )(gain, proj, *pieces)


def pack(tokens, peers):
    frames, patches, width = tokens.shape
    whole = pl.BlockSpec(memory_space=pltpu.VMEM)
    return pl.pallas_call(
        pack_kernel,
        out_shape=[jax.ShapeDtypeStruct((frames * patches // peers, width), tokens.dtype)] * peers,
        in_specs=[whole],
        out_specs=[whole] * peers,
        scratch_shapes=[pltpu.VMEM((width // LANES, frames, patches, LANES), jnp.float32)],
        compiler_params=pltpu.CompilerParams(vmem_limit_bytes=8 * 1024 * 1024),
    )(tokens)


def place(places, pieces, whole, shape, flops):
    anywhere = pl.BlockSpec(memory_space=pl.ANY)
    count = len(pieces)
    others = [] if whole is None else [whole]
    return pl.pallas_call(
        functools.partial(place_kernel, places),
        out_shape=jax.ShapeDtypeStruct(shape, jnp.bfloat16),
        in_specs=[anywhere] * (count + len(others)),
        out_specs=anywhere,
        scratch_shapes=[pltpu.SemaphoreType.DMA] * count,
        input_output_aliases={count: 0} if others else {},
        compiler_params=pltpu.CompilerParams(vmem_limit_bytes=1024 * 1024),
        cost_estimate=pl.CostEstimate(flops=flops, bytes_accessed=flops // 10**4, transcendentals=0),
    )(*pieces, *others)


def exchange(piece, axis, index):
    size = lax.axis_size(axis)
    return lax.ppermute(piece, axis, [(i, i ^ index) for i in range(size)])


def swap(pieces, axis):
    arrived = list(pieces)
    for index in ORDER:
        arrived[index] = exchange(pieces[index], axis, index)
    return arrived


def per_device(
    tokens,
    time_gain,
    time_proj,
    time_out,
    time_scale,
    space_gain,
    space_proj,
    space_out,
    space_scale,
):
    frames, local_count, width = tokens.shape
    peers, sides = lax.axis_size("tm"), lax.axis_size("patch")
    rows = frames * local_count
    all_frames = frames * peers
    time_scale, space_scale, time_gain, space_gain = small(time_scale, space_scale, time_gain, space_gain)
    patches = local_count // peers
    fields = []
    if peers == 8:
        groups = GROUPS
        arrived = swap(pack(tokens, peers), "tm")
        arrived = [[arrived[index] for index in group] for group in groups]
        fields = [project_early(patches, time_gain, time_proj, pieces) for pieces in arrived[:-1]]
        arrived = sum(arrived, [])
    else:
        groups = [[0]]
        outgoing = jnp.swapaxes(tokens.reshape(frames, peers, patches, width), 0, 1).reshape(peers, rows // peers, width)
        arrived = [lax.all_to_all(outgoing, "tm", split_axis=0, concat_axis=0, tiled=True).reshape(rows, width)]
    held = pltpu.VMEM((width // LANES, rows, LANES), jnp.float32)
    space, work = work_space(rows, time_packed(all_frames, patches) * all_frames)
    stream = call(
        functools.partial(time_kernel, groups, patches),
        [((rows, width), jnp.bfloat16)],
        [held, held] + space + work,
        10**10,
        time_scale, time_gain, time_proj, time_out, *fields, *arrived,
    )[0]
    senders = peers * sides
    stream = lax.all_to_all(
        stream.reshape(senders, rows // senders, width), ("tm", "patch"), split_axis=0, concat_axis=0, tiled=True
    ).reshape(rows, width)
    own_frames, columns, half = frames // sides, sides * local_count, sides // 2
    piece = (local_count, width)
    near_rows = half * local_count
    work = [
        pltpu.VMEM((width, near_rows), jnp.bfloat16),
        pltpu.VMEM((HEADS, columns, near_rows), jnp.float32),
        pltpu.VMEM((HEADS, columns, near_rows), jnp.bfloat16),
        pltpu.VMEM((HEADS, 1, near_rows), jnp.float32),
    ]
    far, kept = [], []
    for frame in range(own_frames):
        *pieces, fields, tokens_near = call(
            functools.partial(space_kernel, frame, senders, sides, own_frames),
            [(piece, jnp.bfloat16)] * half
            + [((3 * width, columns), jnp.bfloat16), ((near_rows, width), jnp.float32)],
            [held, pltpu.VMEM((columns, width), jnp.float32)] + work,
            10**10,
            space_scale, space_gain, space_proj, space_out, stream,
        )
        far.append([exchange(piece[None], "patch", half + index) for index, piece in enumerate(pieces)])
        kept += [fields, tokens_near]
    near = call(
        functools.partial(near_kernel, own_frames),
        [((own_frames,) + piece, jnp.bfloat16)] * half,
        work,
        10**6,
        space_scale, space_out, *kept,
    )
    near = [exchange(piece, "patch", index) if index else piece for index, piece in enumerate(near)]
    block = None
    for frame in range(own_frames):
        if frame == own_frames - 1:
            block = place([(index, 0, own_frames) for index in range(half)], near, block, tokens.shape, 10**6)
        places = [(half + index, frame, own_frames) for index in range(half)]
        block = place(places, far[frame], block, tokens.shape, 10**10)
    return block


def solution(mesh):
    in_specs = (P("tm", "patch", None), P(), P(), P(), P(), P(), P(), P(), P())
    out_specs = P("tm", "patch", None)
    return jax.shard_map(
        per_device, mesh=mesh, in_specs=in_specs, out_specs=out_specs, check_vma=False
    )
```

```python
import functools
import math

import jax
import jax.numpy as jnp
from jax import lax
from jax.experimental import pallas as pl
from jax.experimental.pallas import tpu as pltpu
from jax.sharding import PartitionSpec as P

HEADS = 12
HEAD_DIM = 64
WIDTH = HEADS * HEAD_DIM
EPSILON = 1e-06
LOG2_E = math.log2(math.e)
LANES = 128
AHEAD = 12
VMEM_BYTES = 24 * 1024 * 1024

TN = (((0,), (0,)), ((), ()))
TT = (((0,), (1,)), ((), ()))


def dot(left, right, dims=(((1,), (0,)), ((), ()))):
    return lax.dot_general(left, right, dims, preferred_element_type=jnp.float32)


def layer_norm(values, gain):
    centred = values - jnp.mean(values, axis=-1, keepdims=True)
    spread = jnp.mean(centred * centred, axis=-1, keepdims=True)
    return (centred * lax.rsqrt(spread + EPSILON) * gain).astype(jnp.bfloat16)


def unit_columns(fields):
    heads = fields.reshape(HEADS, HEAD_DIM, fields.shape[1])
    squares = jnp.sum(heads * heads, axis=1, keepdims=True)
    return (heads * lax.rsqrt(squares + EPSILON)).reshape(fields.shape)


QUERIES_KEYS = [slice(0, WIDTH), slice(WIDTH, 2 * WIDTH)]
VALUES = [slice(2 * WIDTH, 3 * WIDTH)]


def project(normed, proj_ref, fields_ref, cuts):
    for cut, fields in projected(normed, proj_ref, cuts):
        fields_ref[cut] = fields


def projected(normed, proj_ref, cuts):
    for cut in cuts:
        fields = dot(proj_ref[:, cut], normed, TT)
        if cut.start < 2 * WIDTH:
            fields = unit_columns(fields)
        yield cut, fields.astype(jnp.bfloat16)


def hold(held, values):
    for part in range(held.shape[0]):
        held[part] = values[:, part * LANES : (part + 1) * LANES].astype(jnp.float32)


def pick(held, start, count, step):
    return jnp.concatenate(
        [held[part, pl.ds(start, count, stride=step), :] for part in range(held.shape[0])], axis=1
    )


def head_rows(part, head):
    return slice(part * WIDTH + head * HEAD_DIM, part * WIDTH + (head + 1) * HEAD_DIM)


def attend(fields_ref, scale_ref, mixed_ref, scores_ref, weights_ref, totals_ref, groups, packed, length, project_part):
    span = groups * packed * length
    runs = fields_ref.shape[1] // span
    item_of = (lax.broadcasted_iota(jnp.int32, (1, span), 1) // length) % packed

    def rows(group, item):
        first = (group * packed + item) * length
        return slice(first, first + length)

    def score(at, head):
        cut = slice(at // HEADS * span, (at // HEADS + 1) * span)
        scores_ref[at] = dot(fields_ref[head_rows(1, head), cut], fields_ref[head_rows(0, head), cut], TN)

    def soften(at, head):
        factor = scale_ref[head : head + 1]
        for low in range(0, span, LANES):
            lanes = slice(low, low + LANES)
            mine = jnp.broadcast_to(item_of[:, lanes], (length, LANES))
            scores = []
            for group in range(groups):
                own = scores_ref[at, rows(group, 0), lanes]
                for item in range(1, packed):
                    own = jnp.where(mine == item, scores_ref[at, rows(group, item), lanes], own)
                scores.append(own)
            largest = functools.reduce(jnp.maximum, [jnp.max(own, axis=0, keepdims=True) for own in scores])
            powers = [jnp.exp2((own - largest) * factor) for own in scores]
            totals_ref[at, :, lanes] = 1.0 / sum(jnp.sum(part, axis=0, keepdims=True) for part in powers)
            for group in range(groups):
                for item in range(packed):
                    part = powers[group] if packed == 1 else jnp.where(mine == item, powers[group], 0.0)
                    weights_ref[at, rows(group, item), lanes] = part.astype(jnp.bfloat16)

    def mix(at, head):
        cut = slice(at // HEADS * span, (at // HEADS + 1) * span)
        mixed = dot(fields_ref[head_rows(2, head), cut], weights_ref[at]) * totals_ref[at]
        mixed_ref[head_rows(0, head), cut] = mixed.astype(jnp.bfloat16)

    count = runs * HEADS
    apart = max(1, AHEAD * 256 // span)
    for step in range(count + 2 * apart):
        if step == apart // 2:
            project_part(VALUES)
        for stage, late in ((score, 0), (soften, apart), (mix, 2 * apart)):
            at = step - late
            if 0 <= at < count:
                stage(at, at % HEADS)


def attend_lanes(fields_ref, scale_ref, mixed_ref, scores_ref, weights_ref, totals_ref, lanes):
    for head in range(HEADS):
        scores_ref[head] = dot(fields_ref[head_rows(1, head)], fields_ref[head_rows(0, head), lanes], TN)
    for head in range(HEADS):
        scores = scores_ref[head]
        factor = jnp.broadcast_to(scale_ref[head : head + 1, :1], (1, scores.shape[1]))
        powers = jnp.exp2((scores - jnp.max(scores, axis=0, keepdims=True)) * factor)
        totals_ref[head] = 1.0 / jnp.sum(powers, axis=0, keepdims=True)
        weights_ref[head] = powers.astype(jnp.bfloat16)
    for head in range(HEADS):
        mixed = dot(fields_ref[head_rows(2, head)], weights_ref[head]) * totals_ref[head]
        mixed_ref[head_rows(0, head)] = mixed.astype(jnp.bfloat16)


GROUPS = [[0, 2, 4, 5], [6, 7, 3, 1]]
ORDER = [2, 4, 5, 6, 7, 3, 1]


def pack_kernel(tokens_ref, *refs):
    pieces, held = refs[:-1], refs[-1]
    frames, patches = tokens_ref.shape[0], tokens_ref.shape[1] // len(pieces)
    me = lax.axis_index("tm")
    for frame in range(frames):
        for part in range(held.shape[0]):
            held[part, frame] = tokens_ref[frame, :, part * LANES : (part + 1) * LANES].astype(jnp.float32)
    for index, piece in enumerate(pieces):
        start = pl.multiple_of((me ^ index) * patches, patches)
        for part in range(held.shape[0]):
            rows = [held[part, frame, pl.ds(start, patches)] for frame in range(frames)]
            piece[:, part * LANES : (part + 1) * LANES] = jnp.concatenate(rows, axis=0).astype(jnp.bfloat16)


def hold_pieces(held, pieces):
    start = 0
    for piece in pieces:
        for part in range(held.shape[0]):
            held[part, start : start + piece.shape[0]] = piece[:, part * LANES : (part + 1) * LANES].astype(jnp.float32)
        start += piece.shape[0]


def fields_kernel(patches, gain_ref, proj_ref, *refs):
    pieces, (fields_ref, held) = refs[:-2], refs[-2:]
    hold_pieces(held, pieces)
    tokens = [pick(held, patch, held.shape[1] // patches, patches) for patch in range(patches)]
    project(layer_norm(jnp.concatenate(tokens, axis=0), gain_ref[...]), proj_ref, fields_ref, QUERIES_KEYS + VALUES)


def time_kernel(groups, patches, scale_ref, gain_ref, proj_ref, out_ref, *refs):
    count, ready = sum(map(len, groups)), len(groups) - 1
    fields, pieces = refs[:ready], refs[ready : ready + count]
    stream_ref, held, result, merged, mixed, *work = refs[ready + count :]
    rows = held.shape[1] // len(groups)
    length = rows // patches
    packed = time_packed(len(groups) * length, patches)
    hold_pieces(held, pieces)
    turn = len(groups) == 2
    order = [patch ^ packed if turn else patch for patch in range(patches)]
    tokens = [pick(held, ready * rows + patch, length, patches) for patch in order]
    normed = layer_norm(jnp.concatenate(tokens, axis=0), gain_ref[...])

    def project_part(cuts):
        if not turn:
            return project(normed, proj_ref, merged, cuts)
        for cut, own in projected(normed, proj_ref, cuts):
            near = lax.broadcasted_iota(jnp.int32, (cut.stop - cut.start, LANES), 1) < packed * length
            for tile in range(0, rows, LANES):
                first, second = fields[0][cut, tile : tile + LANES], own[:, tile : tile + LANES]
                merged[cut, 2 * tile : 2 * tile + LANES] = jnp.where(near, first, second)
                merged[cut, 2 * tile + LANES : 2 * tile + 2 * LANES] = jnp.where(near, second, first)

    project_part(QUERIES_KEYS)
    attend(merged, scale_ref, mixed, *work, len(groups), packed, length, project_part)
    half = max(patches // 2, packed)
    for patch in range(patches):
        if patch % half == 0:
            cut = slice(patch * len(groups) * length, (patch + half) * len(groups) * length)
            update = dot(mixed[:, cut], out_ref[...], TN)
        for group in range(len(groups)):
            unit = patch % half // packed
            slot = group ^ (unit % 2) if turn else group
            first = ((unit * len(groups) + slot) * packed + patch % packed) * length
            place = pl.ds(group * rows + patch, length, stride=patches)
            for part in range(result.shape[0]):
                lanes = slice(part * LANES, (part + 1) * LANES)
                result[part, place, :] = held[part, place, :] + update[first : first + length, lanes]
    me = lax.axis_index("tm")
    size = pieces[0].shape[0]
    for index, piece in enumerate(place for group in groups for place in group):
        start = 0 if count == 1 else pl.multiple_of((me ^ piece) * size, size)
        for part in range(result.shape[0]):
            values = result[part, index * size : (index + 1) * size]
            stream_ref[pl.ds(start, size), part * LANES : (part + 1) * LANES] = values.astype(jnp.bfloat16)


def space_kernel(
    frame, senders, sides, frames, scale_ref, gain_ref, proj_ref, out_ref, stream_ref, *refs
):
    pieces, (fields, kept, held, tokens, mixed, *work) = refs[: sides // 2], refs[sides // 2 :]
    side_patches = pieces[0].shape[0]
    piece = stream_ref.shape[0] // senders // frames
    me = lax.axis_index("patch")
    if piece % 8:
        hold(held, stream_ref)
    for index in range(sides):
        first = index * side_patches
        if piece % 8:
            rows = pick(held, ((me ^ index) * frames + frame) * piece, senders // sides, sides * frames)
            tokens[first : first + side_patches] = rows
        else:
            for sender in range(senders // sides):
                start = pl.multiple_of((sender * sides + (me ^ index)) * frames * piece, frames * piece)
                rows = stream_ref[pl.ds(start, frames * piece), :].astype(jnp.float32)
                place = first + sender * piece
                tokens[place : place + piece] = rows[frame * piece : (frame + 1) * piece]
    half = sides // 2 * side_patches
    project(layer_norm(tokens[...], gain_ref[...]), proj_ref, fields, QUERIES_KEYS + VALUES)
    attend_lanes(fields, scale_ref, mixed, *work, slice(half, 2 * half))
    stream = tokens[half:] + dot(mixed[...], out_ref[...], TN)
    for index, target in enumerate(pieces):
        target[...] = stream[index * side_patches : (index + 1) * side_patches].astype(jnp.bfloat16)
    kept[...] = tokens[:half].astype(jnp.bfloat16)


def near_kernel(frames, scale_ref, out_ref, *refs):
    pieces, (mixed, *work) = refs[2 * frames : -4], refs[-4:]
    side_patches = pieces[0].shape[1]
    for frame in range(frames):
        fields, kept = refs[2 * frame : 2 * frame + 2]
        attend_lanes(fields, scale_ref, mixed, *work, slice(0, kept.shape[0]))
        stream = kept[...].astype(jnp.float32) + dot(mixed[...], out_ref[...], TN)
        for index, target in enumerate(pieces):
            target[frame] = stream[index * side_patches : (index + 1) * side_patches].astype(jnp.bfloat16)


def place_kernel(places, *refs):
    count = len(places)
    pieces, whole, sems = refs[:count], refs[-count - 1], refs[-count:]
    me = lax.axis_index("patch")
    copies = [
        pltpu.make_async_copy(piece, whole.at[pl.ds((me ^ index) * frames + first, piece.shape[0])], sem)
        for piece, (index, first, frames), sem in zip(pieces, places, sems)
    ]
    for copy in copies:
        copy.start()
    for copy in copies:
        copy.wait()


def time_packed(frames, patches):
    return max(1, min(patches, LANES // frames))


def work_space(rows, span):
    return [
        pltpu.VMEM((3 * WIDTH, rows), jnp.bfloat16),
        pltpu.VMEM((WIDTH, rows), jnp.bfloat16),
    ], [
        pltpu.VMEM((rows // span * HEADS, span, span), jnp.float32),
        pltpu.VMEM((rows // span * HEADS, span, span), jnp.bfloat16),
        pltpu.VMEM((rows // span * HEADS, 1, span), jnp.float32),
    ]


def small_kernel(packed_ref, time_scale_ref, space_scale_ref, time_gain_ref, space_gain_ref):
    time_gain_ref[...] = packed_ref[:, :WIDTH]
    space_gain_ref[...] = packed_ref[:, WIDTH : 2 * WIDTH]
    for index, target in enumerate((time_scale_ref, space_scale_ref)):
        for head in range(HEADS):
            place = 2 * WIDTH + index * HEADS + head
            target[head : head + 1] = jnp.broadcast_to(packed_ref[:, place : place + 1] * LOG2_E, (1, LANES))


def small(time_scale, space_scale, time_gain, space_gain):
    whole = pl.BlockSpec(memory_space=pltpu.VMEM)
    shapes = [(HEADS, LANES), (HEADS, LANES), (1, WIDTH), (1, WIDTH)]
    return pl.pallas_call(
        small_kernel,
        out_shape=[jax.ShapeDtypeStruct(shape, jnp.float32) for shape in shapes],
        in_specs=[whole],
        out_specs=[whole] * 4,
        compiler_params=pltpu.CompilerParams(vmem_limit_bytes=1024 * 1024),
        cost_estimate=pl.CostEstimate(flops=10**10, bytes_accessed=10**5, transcendentals=0),
    )(jnp.concatenate([time_gain, space_gain, time_scale, space_scale])[None])


def call(kernel, out_shapes, scratch, flops, *rows):
    whole = pl.BlockSpec(memory_space=pltpu.VMEM)
    return pl.pallas_call(
        kernel,
        out_shape=[jax.ShapeDtypeStruct(*shape) for shape in out_shapes],
        in_specs=[whole] * len(rows),
        out_specs=[whole] * len(out_shapes),
        scratch_shapes=scratch,
        compiler_params=pltpu.CompilerParams(vmem_limit_bytes=VMEM_BYTES),
        cost_estimate=pl.CostEstimate(flops=flops, bytes_accessed=flops // 1000, transcendentals=0),
    )(*rows)


def project_early(patches, gain, proj, pieces):
    whole = pl.BlockSpec(memory_space=pltpu.VMEM)
    rows = sum(piece.shape[0] for piece in pieces)
    return pl.pallas_call(
        functools.partial(fields_kernel, patches),
        out_shape=jax.ShapeDtypeStruct((3 * WIDTH, rows), jnp.bfloat16),
        in_specs=[whole] * (2 + len(pieces)),
        out_specs=whole,
        scratch_shapes=[pltpu.VMEM((WIDTH // LANES, rows, LANES), jnp.float32)],
        compiler_params=pltpu.CompilerParams(vmem_limit_bytes=VMEM_BYTES),
        cost_estimate=pl.CostEstimate(flops=5 * 10**9, bytes_accessed=7 * 10**6, transcendentals=10**6),
    )(gain, proj, *pieces)


def pack(tokens, peers):
    frames, patches, width = tokens.shape
    whole = pl.BlockSpec(memory_space=pltpu.VMEM)
    return pl.pallas_call(
        pack_kernel,
        out_shape=[jax.ShapeDtypeStruct((frames * patches // peers, width), tokens.dtype)] * peers,
        in_specs=[whole],
        out_specs=[whole] * peers,
        scratch_shapes=[pltpu.VMEM((width // LANES, frames, patches, LANES), jnp.float32)],
        compiler_params=pltpu.CompilerParams(vmem_limit_bytes=8 * 1024 * 1024),
    )(tokens)


def place(places, pieces, whole, shape, flops):
    anywhere = pl.BlockSpec(memory_space=pl.ANY)
    count = len(pieces)
    others = [] if whole is None else [whole]
    return pl.pallas_call(
        functools.partial(place_kernel, places),
        out_shape=jax.ShapeDtypeStruct(shape, jnp.bfloat16),
        in_specs=[anywhere] * (count + len(others)),
        out_specs=anywhere,
        scratch_shapes=[pltpu.SemaphoreType.DMA] * count,
        input_output_aliases={count: 0} if others else {},
        compiler_params=pltpu.CompilerParams(vmem_limit_bytes=1024 * 1024),
        cost_estimate=pl.CostEstimate(flops=flops, bytes_accessed=flops // 10**4, transcendentals=0),
    )(*pieces, *others)


def exchange(piece, axis, index):
    size = lax.axis_size(axis)
    return lax.ppermute(piece, axis, [(i, i ^ index) for i in range(size)])


def swap(pieces, axis):
    arrived = list(pieces)
    for index in ORDER:
        arrived[index] = exchange(pieces[index], axis, index)
    return arrived


def per_device(
    tokens,
    time_gain,
    time_proj,
    time_out,
    time_scale,
    space_gain,
    space_proj,
    space_out,
    space_scale,
):
    frames, local_count, width = tokens.shape
    peers, sides = lax.axis_size("tm"), lax.axis_size("patch")
    rows = frames * local_count
    all_frames = frames * peers
    time_scale, space_scale, time_gain, space_gain = small(time_scale, space_scale, time_gain, space_gain)
    patches = local_count // peers
    fields = []
    if peers == 8:
        groups = GROUPS
        arrived = swap(pack(tokens, peers), "tm")
        arrived = [[arrived[index] for index in group] for group in groups]
        fields = [project_early(patches, time_gain, time_proj, pieces) for pieces in arrived[:-1]]
        arrived = sum(arrived, [])
    else:
        groups = [[0]]
        outgoing = jnp.swapaxes(tokens.reshape(frames, peers, patches, width), 0, 1).reshape(peers, rows // peers, width)
        arrived = [lax.all_to_all(outgoing, "tm", split_axis=0, concat_axis=0, tiled=True).reshape(rows, width)]
    held = pltpu.VMEM((width // LANES, rows, LANES), jnp.float32)
    space, work = work_space(rows, time_packed(all_frames, patches) * all_frames)
    stream = call(
        functools.partial(time_kernel, groups, patches),
        [((rows, width), jnp.bfloat16)],
        [held, held] + space + work,
        10**10,
        time_scale, time_gain, time_proj, time_out, *fields, *arrived,
    )[0]
    senders = peers * sides
    stream = lax.all_to_all(
        stream.reshape(senders, rows // senders, width), ("tm", "patch"), split_axis=0, concat_axis=0, tiled=True
    ).reshape(rows, width)
    own_frames, columns, half = frames // sides, sides * local_count, sides // 2
    piece = (local_count, width)
    near_rows = half * local_count
    work = [
        pltpu.VMEM((width, near_rows), jnp.bfloat16),
        pltpu.VMEM((HEADS, columns, near_rows), jnp.float32),
        pltpu.VMEM((HEADS, columns, near_rows), jnp.bfloat16),
        pltpu.VMEM((HEADS, 1, near_rows), jnp.float32),
    ]
    far, kept = [], []
    for frame in range(own_frames):
        *pieces, fields, tokens_near = call(
            functools.partial(space_kernel, frame, senders, sides, own_frames),
            [(piece, jnp.bfloat16)] * half
            + [((3 * width, columns), jnp.bfloat16), ((near_rows, width), jnp.bfloat16)],
            [held, pltpu.VMEM((columns, width), jnp.float32)] + work,
            10**10,
            space_scale, space_gain, space_proj, space_out, stream,
        )
        far.append([exchange(piece[None], "patch", half + index) for index, piece in enumerate(pieces)])
        kept += [fields, tokens_near]
    near = call(
        functools.partial(near_kernel, own_frames),
        [((own_frames,) + piece, jnp.bfloat16)] * half,
        work,
        10**6,
        space_scale, space_out, *kept,
    )
    near = [exchange(piece, "patch", index) if index else piece for index, piece in enumerate(near)]
    block = None
    for frame in range(own_frames):
        if frame == own_frames - 1:
            block = place([(index, 0, own_frames) for index in range(half)], near, block, tokens.shape, 10**6)
        places = [(half + index, frame, own_frames) for index in range(half)]
        block = place(places, far[frame], block, tokens.shape, 10**10)
    return block


def solution(mesh):
    in_specs = (P("tm", "patch", None), P(), P(), P(), P(), P(), P(), P(), P())
    out_specs = P("tm", "patch", None)
    return jax.shard_map(
        per_device, mesh=mesh, in_specs=in_specs, out_specs=out_specs, check_vma=False
    )
```

```python
import functools
import math

import jax
import jax.numpy as jnp
from jax import lax
from jax.experimental import pallas as pl
from jax.experimental.pallas import tpu as pltpu
from jax.sharding import PartitionSpec as P

HEADS = 12
HEAD_DIM = 64
WIDTH = HEADS * HEAD_DIM
EPSILON = 1e-06
LOG2_E = math.log2(math.e)
LANES = 128
AHEAD = 24
VMEM_BYTES = 24 * 1024 * 1024

TN = (((0,), (0,)), ((), ()))
TT = (((0,), (1,)), ((), ()))


def dot(left, right, dims=(((1,), (0,)), ((), ()))):
    return lax.dot_general(left, right, dims, preferred_element_type=jnp.float32)


def layer_norm(values, gain):
    centred = values - jnp.mean(values, axis=-1, keepdims=True)
    spread = jnp.mean(centred * centred, axis=-1, keepdims=True)
    return (centred * lax.rsqrt(spread + EPSILON) * gain).astype(jnp.bfloat16)


def unit_columns(fields):
    heads = fields.reshape(HEADS, HEAD_DIM, fields.shape[1])
    squares = jnp.sum(heads * heads, axis=1, keepdims=True)
    return (heads * lax.rsqrt(squares + EPSILON)).reshape(fields.shape)


QUERIES_KEYS = [slice(0, WIDTH), slice(WIDTH, 2 * WIDTH)]
VALUES = [slice(2 * WIDTH, 3 * WIDTH)]


def project(normed, proj_ref, fields_ref, cuts):
    for cut, fields in projected(normed, proj_ref, cuts):
        fields_ref[cut] = fields


def projected(normed, proj_ref, cuts):
    for cut in cuts:
        fields = dot(proj_ref[:, cut], normed, TT)
        if cut.start < 2 * WIDTH:
            fields = unit_columns(fields)
        yield cut, fields.astype(jnp.bfloat16)


def hold(held, values):
    for part in range(held.shape[0]):
        held[part] = values[:, part * LANES : (part + 1) * LANES].astype(jnp.float32)


def pick(held, start, count, step):
    return jnp.concatenate(
        [held[part, pl.ds(start, count, stride=step), :] for part in range(held.shape[0])], axis=1
    )


def head_rows(part, head):
    return slice(part * WIDTH + head * HEAD_DIM, part * WIDTH + (head + 1) * HEAD_DIM)


def attend(fields_ref, scale_ref, mixed_ref, scores_ref, weights_ref, totals_ref, groups, packed, length, project_part):
    span = groups * packed * length
    runs = fields_ref.shape[1] // span
    item_of = (lax.broadcasted_iota(jnp.int32, (1, span), 1) // length) % packed

    def rows(group, item):
        first = (group * packed + item) * length
        return slice(first, first + length)

    def score(at, head):
        cut = slice(at // HEADS * span, (at // HEADS + 1) * span)
        scores_ref[at] = dot(fields_ref[head_rows(1, head), cut], fields_ref[head_rows(0, head), cut], TN)

    def soften(at, head):
        factor = scale_ref[head : head + 1]
        for low in range(0, span, LANES):
            lanes = slice(low, low + LANES)
            mine = jnp.broadcast_to(item_of[:, lanes], (length, LANES))
            scores = []
            for group in range(groups):
                own = scores_ref[at, rows(group, 0), lanes]
                for item in range(1, packed):
                    own = jnp.where(mine == item, scores_ref[at, rows(group, item), lanes], own)
                scores.append(own)
            largest = functools.reduce(jnp.maximum, [jnp.max(own, axis=0, keepdims=True) for own in scores])
            powers = [jnp.exp2((own - largest) * factor) for own in scores]
            totals_ref[at, :, lanes] = 1.0 / sum(jnp.sum(part, axis=0, keepdims=True) for part in powers)
            for group in range(groups):
                for item in range(packed):
                    part = powers[group] if packed == 1 else jnp.where(mine == item, powers[group], 0.0)
                    weights_ref[at, rows(group, item), lanes] = part.astype(jnp.bfloat16)

    def mix(at, head):
        cut = slice(at // HEADS * span, (at // HEADS + 1) * span)
        mixed = dot(fields_ref[head_rows(2, head), cut], weights_ref[at]) * totals_ref[at]
        mixed_ref[head_rows(0, head), cut] = mixed.astype(jnp.bfloat16)

    count = runs * HEADS
    apart = max(1, AHEAD * 256 // span)
    for step in range(count + 2 * apart):
        if step == apart // 2:
            project_part(VALUES)
        for stage, late in ((score, 0), (soften, apart), (mix, 2 * apart)):
            at = step - late
            if 0 <= at < count:
                stage(at, at % HEADS)


def attend_lanes(fields_ref, scale_ref, mixed_ref, scores_ref, weights_ref, totals_ref, lanes):
    for head in range(HEADS):
        scores_ref[head] = dot(fields_ref[head_rows(1, head)], fields_ref[head_rows(0, head), lanes], TN)
    for head in range(HEADS):
        scores = scores_ref[head]
        factor = jnp.broadcast_to(scale_ref[head : head + 1, :1], (1, scores.shape[1]))
        powers = jnp.exp2((scores - jnp.max(scores, axis=0, keepdims=True)) * factor)
        totals_ref[head] = 1.0 / jnp.sum(powers, axis=0, keepdims=True)
        weights_ref[head] = powers.astype(jnp.bfloat16)
    for head in range(HEADS):
        mixed = dot(fields_ref[head_rows(2, head)], weights_ref[head]) * totals_ref[head]
        mixed_ref[head_rows(0, head)] = mixed.astype(jnp.bfloat16)


GROUPS = [[0, 2, 4, 5], [6, 7, 3, 1]]
ORDER = [2, 4, 5, 6, 7, 3, 1]


def pack_kernel(tokens_ref, *refs):
    pieces, held = refs[:-1], refs[-1]
    frames, patches = tokens_ref.shape[0], tokens_ref.shape[1] // len(pieces)
    me = lax.axis_index("tm")
    for frame in range(frames):
        for part in range(held.shape[0]):
            held[part, frame] = tokens_ref[frame, :, part * LANES : (part + 1) * LANES].astype(jnp.float32)
    for index, piece in enumerate(pieces):
        start = pl.multiple_of((me ^ index) * patches, patches)
        for part in range(held.shape[0]):
            rows = [held[part, frame, pl.ds(start, patches)] for frame in range(frames)]
            piece[:, part * LANES : (part + 1) * LANES] = jnp.concatenate(rows, axis=0).astype(jnp.bfloat16)


def hold_pieces(held, pieces):
    start = 0
    for piece in pieces:
        for part in range(held.shape[0]):
            held[part, start : start + piece.shape[0]] = piece[:, part * LANES : (part + 1) * LANES].astype(jnp.float32)
        start += piece.shape[0]


def fields_kernel(patches, gain_ref, proj_ref, *refs):
    pieces, (fields_ref, held) = refs[:-2], refs[-2:]
    hold_pieces(held, pieces)
    tokens = [pick(held, patch, held.shape[1] // patches, patches) for patch in range(patches)]
    project(layer_norm(jnp.concatenate(tokens, axis=0), gain_ref[...]), proj_ref, fields_ref, QUERIES_KEYS + VALUES)


def time_kernel(groups, patches, scale_ref, gain_ref, proj_ref, out_ref, *refs):
    count, ready = sum(map(len, groups)), len(groups) - 1
    fields, pieces = refs[:ready], refs[ready : ready + count]
    stream_ref, held, result, merged, mixed, *work = refs[ready + count :]
    rows = held.shape[1] // len(groups)
    length = rows // patches
    packed = time_packed(len(groups) * length, patches)
    hold_pieces(held, pieces)
    turn = len(groups) == 2
    order = [patch ^ packed if turn else patch for patch in range(patches)]
    tokens = [pick(held, ready * rows + patch, length, patches) for patch in order]
    normed = layer_norm(jnp.concatenate(tokens, axis=0), gain_ref[...])

    def project_part(cuts):
        if not turn:
            return project(normed, proj_ref, merged, cuts)
        for cut, own in projected(normed, proj_ref, cuts):
            near = lax.broadcasted_iota(jnp.int32, (cut.stop - cut.start, LANES), 1) < packed * length
            for tile in range(0, rows, LANES):
                first, second = fields[0][cut, tile : tile + LANES], own[:, tile : tile + LANES]
                merged[cut, 2 * tile : 2 * tile + LANES] = jnp.where(near, first, second)
                merged[cut, 2 * tile + LANES : 2 * tile + 2 * LANES] = jnp.where(near, second, first)

    project_part(QUERIES_KEYS)
    attend(merged, scale_ref, mixed, *work, len(groups), packed, length, project_part)
    half = max(patches // 2, packed)
    for patch in range(patches):
        if patch % half == 0:
            cut = slice(patch * len(groups) * length, (patch + half) * len(groups) * length)
            update = dot(mixed[:, cut], out_ref[...], TN)
        for group in range(len(groups)):
            unit = patch % half // packed
            slot = group ^ (unit % 2) if turn else group
            first = ((unit * len(groups) + slot) * packed + patch % packed) * length
            place = pl.ds(group * rows + patch, length, stride=patches)
            for part in range(result.shape[0]):
                lanes = slice(part * LANES, (part + 1) * LANES)
                result[part, place, :] = held[part, place, :] + update[first : first + length, lanes]
    me = lax.axis_index("tm")
    size = pieces[0].shape[0]
    for index, piece in enumerate(place for group in groups for place in group):
        start = 0 if count == 1 else pl.multiple_of((me ^ piece) * size, size)
        for part in range(result.shape[0]):
            values = result[part, index * size : (index + 1) * size]
            stream_ref[pl.ds(start, size), part * LANES : (part + 1) * LANES] = values.astype(jnp.bfloat16)


def space_kernel(
    frame, senders, sides, frames, scale_ref, gain_ref, proj_ref, out_ref, stream_ref, *refs
):
    pieces, (fields, kept, held, tokens, mixed, *work) = refs[: sides // 2], refs[sides // 2 :]
    side_patches = pieces[0].shape[0]
    piece = stream_ref.shape[0] // senders // frames
    me = lax.axis_index("patch")
    if piece % 8:
        hold(held, stream_ref)
    for index in range(sides):
        first = index * side_patches
        if piece % 8:
            rows = pick(held, ((me ^ index) * frames + frame) * piece, senders // sides, sides * frames)
            tokens[first : first + side_patches] = rows
        else:
            for sender in range(senders // sides):
                start = pl.multiple_of((sender * sides + (me ^ index)) * frames * piece, frames * piece)
                rows = stream_ref[pl.ds(start, frames * piece), :].astype(jnp.float32)
                place = first + sender * piece
                tokens[place : place + piece] = rows[frame * piece : (frame + 1) * piece]
    half = sides // 2 * side_patches
    project(layer_norm(tokens[...], gain_ref[...]), proj_ref, fields, QUERIES_KEYS + VALUES)
    attend_lanes(fields, scale_ref, mixed, *work, slice(half, 2 * half))
    stream = tokens[half:] + dot(mixed[...], out_ref[...], TN)
    for index, target in enumerate(pieces):
        target[...] = stream[index * side_patches : (index + 1) * side_patches].astype(jnp.bfloat16)
    kept[...] = tokens[:half]


def near_kernel(frames, scale_ref, out_ref, *refs):
    pieces, (mixed, *work) = refs[2 * frames : -4], refs[-4:]
    side_patches = pieces[0].shape[1]
    for frame in range(frames):
        fields, kept = refs[2 * frame : 2 * frame + 2]
        attend_lanes(fields, scale_ref, mixed, *work, slice(0, kept.shape[0]))
        stream = kept[...] + dot(mixed[...], out_ref[...], TN)
        for index, target in enumerate(pieces):
            target[frame] = stream[index * side_patches : (index + 1) * side_patches].astype(jnp.bfloat16)


def place_kernel(places, *refs):
    count = len(places)
    pieces, whole, sems = refs[:count], refs[-count - 1], refs[-count:]
    me = lax.axis_index("patch")
    copies = [
        pltpu.make_async_copy(piece, whole.at[pl.ds((me ^ index) * frames + first, piece.shape[0])], sem)
        for piece, (index, first, frames), sem in zip(pieces, places, sems)
    ]
    for copy in copies:
        copy.start()
    for copy in copies:
        copy.wait()


def time_packed(frames, patches):
    return max(1, min(patches, LANES // frames))


def work_space(rows, span):
    return [
        pltpu.VMEM((3 * WIDTH, rows), jnp.bfloat16),
        pltpu.VMEM((WIDTH, rows), jnp.bfloat16),
    ], [
        pltpu.VMEM((rows // span * HEADS, span, span), jnp.float32),
        pltpu.VMEM((rows // span * HEADS, span, span), jnp.bfloat16),
        pltpu.VMEM((rows // span * HEADS, 1, span), jnp.float32),
    ]


def small_kernel(packed_ref, time_scale_ref, space_scale_ref, time_gain_ref, space_gain_ref):
    time_gain_ref[...] = packed_ref[:, :WIDTH]
    space_gain_ref[...] = packed_ref[:, WIDTH : 2 * WIDTH]
    for index, target in enumerate((time_scale_ref, space_scale_ref)):
        for head in range(HEADS):
            place = 2 * WIDTH + index * HEADS + head
            target[head : head + 1] = jnp.broadcast_to(packed_ref[:, place : place + 1] * LOG2_E, (1, LANES))


def small(time_scale, space_scale, time_gain, space_gain):
    whole = pl.BlockSpec(memory_space=pltpu.VMEM)
    shapes = [(HEADS, LANES), (HEADS, LANES), (1, WIDTH), (1, WIDTH)]
    return pl.pallas_call(
        small_kernel,
        out_shape=[jax.ShapeDtypeStruct(shape, jnp.float32) for shape in shapes],
        in_specs=[whole],
        out_specs=[whole] * 4,
        compiler_params=pltpu.CompilerParams(vmem_limit_bytes=1024 * 1024),
        cost_estimate=pl.CostEstimate(flops=10**10, bytes_accessed=10**5, transcendentals=0),
    )(jnp.concatenate([time_gain, space_gain, time_scale, space_scale])[None])


def call(kernel, out_shapes, scratch, flops, *rows):
    whole = pl.BlockSpec(memory_space=pltpu.VMEM)
    return pl.pallas_call(
        kernel,
        out_shape=[jax.ShapeDtypeStruct(*shape) for shape in out_shapes],
        in_specs=[whole] * len(rows),
        out_specs=[whole] * len(out_shapes),
        scratch_shapes=scratch,
        compiler_params=pltpu.CompilerParams(vmem_limit_bytes=VMEM_BYTES),
        cost_estimate=pl.CostEstimate(flops=flops, bytes_accessed=flops // 1000, transcendentals=0),
    )(*rows)


def project_early(patches, gain, proj, pieces):
    whole = pl.BlockSpec(memory_space=pltpu.VMEM)
    rows = sum(piece.shape[0] for piece in pieces)
    return pl.pallas_call(
        functools.partial(fields_kernel, patches),
        out_shape=jax.ShapeDtypeStruct((3 * WIDTH, rows), jnp.bfloat16),
        in_specs=[whole] * (2 + len(pieces)),
        out_specs=whole,
        scratch_shapes=[pltpu.VMEM((WIDTH // LANES, rows, LANES), jnp.float32)],
        compiler_params=pltpu.CompilerParams(vmem_limit_bytes=VMEM_BYTES),
        cost_estimate=pl.CostEstimate(flops=5 * 10**9, bytes_accessed=7 * 10**6, transcendentals=10**6),
    )(gain, proj, *pieces)


def pack(tokens, peers):
    frames, patches, width = tokens.shape
    whole = pl.BlockSpec(memory_space=pltpu.VMEM)
    return pl.pallas_call(
        pack_kernel,
        out_shape=[jax.ShapeDtypeStruct((frames * patches // peers, width), tokens.dtype)] * peers,
        in_specs=[whole],
        out_specs=[whole] * peers,
        scratch_shapes=[pltpu.VMEM((width // LANES, frames, patches, LANES), jnp.float32)],
        compiler_params=pltpu.CompilerParams(vmem_limit_bytes=8 * 1024 * 1024),
    )(tokens)


def place(places, pieces, whole, shape, flops):
    anywhere = pl.BlockSpec(memory_space=pl.ANY)
    count = len(pieces)
    others = [] if whole is None else [whole]
    return pl.pallas_call(
        functools.partial(place_kernel, places),
        out_shape=jax.ShapeDtypeStruct(shape, jnp.bfloat16),
        in_specs=[anywhere] * (count + len(others)),
        out_specs=anywhere,
        scratch_shapes=[pltpu.SemaphoreType.DMA] * count,
        input_output_aliases={count: 0} if others else {},
        compiler_params=pltpu.CompilerParams(vmem_limit_bytes=1024 * 1024),
        cost_estimate=pl.CostEstimate(flops=flops, bytes_accessed=flops // 10**4, transcendentals=0),
    )(*pieces, *others)


def exchange(piece, axis, index):
    size = lax.axis_size(axis)
    return lax.ppermute(piece, axis, [(i, i ^ index) for i in range(size)])


def swap(pieces, axis):
    arrived = list(pieces)
    for index in ORDER:
        arrived[index] = exchange(pieces[index], axis, index)
    return arrived


def per_device(
    tokens,
    time_gain,
    time_proj,
    time_out,
    time_scale,
    space_gain,
    space_proj,
    space_out,
    space_scale,
):
    frames, local_count, width = tokens.shape
    peers, sides = lax.axis_size("tm"), lax.axis_size("patch")
    rows = frames * local_count
    all_frames = frames * peers
    time_scale, space_scale, time_gain, space_gain = small(time_scale, space_scale, time_gain, space_gain)
    patches = local_count // peers
    fields = []
    if peers == 8:
        groups = GROUPS
        arrived = swap(pack(tokens, peers), "tm")
        arrived = [[arrived[index] for index in group] for group in groups]
        fields = [project_early(patches, time_gain, time_proj, pieces) for pieces in arrived[:-1]]
        arrived = sum(arrived, [])
    else:
        groups = [[0]]
        outgoing = jnp.swapaxes(tokens.reshape(frames, peers, patches, width), 0, 1).reshape(peers, rows // peers, width)
        arrived = [lax.all_to_all(outgoing, "tm", split_axis=0, concat_axis=0, tiled=True).reshape(rows, width)]
    held = pltpu.VMEM((width // LANES, rows, LANES), jnp.float32)
    space, work = work_space(rows, time_packed(all_frames, patches) * all_frames)
    stream = call(
        functools.partial(time_kernel, groups, patches),
        [((rows, width), jnp.bfloat16)],
        [held, held] + space + work,
        10**10,
        time_scale, time_gain, time_proj, time_out, *fields, *arrived,
    )[0]
    senders = peers * sides
    stream = lax.all_to_all(
        stream.reshape(senders, rows // senders, width), ("tm", "patch"), split_axis=0, concat_axis=0, tiled=True
    ).reshape(rows, width)
    own_frames, columns, half = frames // sides, sides * local_count, sides // 2
    piece = (local_count, width)
    near_rows = half * local_count
    work = [
        pltpu.VMEM((width, near_rows), jnp.bfloat16),
        pltpu.VMEM((HEADS, columns, near_rows), jnp.float32),
        pltpu.VMEM((HEADS, columns, near_rows), jnp.bfloat16),
        pltpu.VMEM((HEADS, 1, near_rows), jnp.float32),
    ]
    far, kept = [], []
    for frame in range(own_frames):
        *pieces, fields, tokens_near = call(
            functools.partial(space_kernel, frame, senders, sides, own_frames),
            [(piece, jnp.bfloat16)] * half
            + [((3 * width, columns), jnp.bfloat16), ((near_rows, width), jnp.float32)],
            [held, pltpu.VMEM((columns, width), jnp.float32)] + work,
            10**10,
            space_scale, space_gain, space_proj, space_out, stream,
        )
        far.append([exchange(piece[None], "patch", half + index) for index, piece in enumerate(pieces)])
        kept += [fields, tokens_near]
    near = call(
        functools.partial(near_kernel, own_frames),
        [((own_frames,) + piece, jnp.bfloat16)] * half,
        work,
        10**6,
        space_scale, space_out, *kept,
    )
    near = [exchange(piece, "patch", index) if index else piece for index, piece in enumerate(near)]
    block = None
    for frame in range(own_frames):
        if frame == own_frames - 1:
            block = place([(index, 0, own_frames) for index in range(half)], near, block, tokens.shape, 10**6)
        places = [(half + index, frame, own_frames) for index in range(half)]
        block = place(places, far[frame], block, tokens.shape, 10**10)
    return block


def solution(mesh):
    in_specs = (P("tm", "patch", None), P(), P(), P(), P(), P(), P(), P(), P())
    out_specs = P("tm", "patch", None)
    return jax.shard_map(
        per_device, mesh=mesh, in_specs=in_specs, out_specs=out_specs, check_vma=False
    )
```
